32 devices in a mesh: dp: 4 (over z), pair: 8 (over y, x, core).
Axes of the slice: x: 2, y: 2, z: 4, core: 2. Of those that a mesh axis runs over, the one named last changes fastest.
Arguments:
- embeddings: bfloat16 [128, 512, 256], P('pair', 'dp'), may hold values from -6 to 6
- field_width: int32 [128], replicated, may hold values from 64 to 256, as said below
- pair_fields: int32 [384, 2], replicated, may hold values from 0 to 127, as said below
- pair_mats: bfloat16 [384, 256, 256], P('pair'), may hold values from -0.0048828125 to 0.0048828125
- labels: int32 [512], P('dp'), may hold values 0 or 1
Outputs:
- logits: float32 [512], P('dp')
- mat_grad: bfloat16 [384, 256, 256], P('pair', 'dp')
- emb_grad: float32 [128, 512, 256], P('pair', 'dp')
The draws below stay inside these ranges and needn't reach their ends.
Inputs may be any that keep to these rules, and one draw needn't show every extreme that they name: `field_width`: each is 64, 128 or 256. `pair_fields`: the two fields of a pair differ. The 48 pairs of one owner read at most 3 different fields from the 16 fields of any one owner (field f is owned by index f // 16), and exactly 3 from some owner.
All inputs are finite; a program needn't handle non-finite values. No bound on the sum of `labels` on one device may be relied on, other than what follows from the above.
Results may differ from the reference program's by a relative error of at most 0.017.
Values may be sent and summed in bfloat16 or wider, within the bound.
No kernel may reach another device: no remote copies, remote signals or barrier semaphores. Data moves between devices by JAX's collectives and lax.ppermute only.
A program may use at most 128 MiB of HBM per device.

```python
import jax
import jax.numpy as jnp
from jax import lax

D = 256
FIELD_DEV = 16
CAP = 3
PAIR_DEV = 48
SAMP_DEV = 128
FIELDS = 128
PAIRS = 384
SAMPLES = 512


def draw_field_width(key, part):
    choose = jax.random.randint(key, (FIELDS,), 0, 3)
    return jnp.where(choose == 0, D // 4, jnp.where(choose == 1, D // 2, D)).astype(jnp.int32)


def draw_pair_fields(key, part):
    owners = PAIRS // PAIR_DEV
    key_pick = jax.random.fold_in(key, 11)
    key_offset = jax.random.fold_in(key, 23)
    scores = jax.random.randint(key_pick, (owners, owners, FIELD_DEV), 0, 1 << 20)
    scores = scores * FIELD_DEV + jnp.arange(FIELD_DEV, dtype=jnp.int32)[None, None, :]
    picks = jnp.argsort(scores, axis=-1)[:, :, :CAP].astype(jnp.int32)
    field_pool = jnp.arange(owners, dtype=jnp.int32)[None, :, None] * FIELD_DEV + picks
    field_pool = field_pool.reshape(owners, owners * CAP)
    slots_total = owners * CAP
    position = jnp.arange(PAIR_DEV, dtype=jnp.int32)
    first_slot = jnp.broadcast_to(position % slots_total, (owners, PAIR_DEV))
    offset = jax.random.randint(key_offset, (owners, PAIR_DEV), 0, slots_total - 1)
    second_slot = (first_slot + 1 + offset) % slots_total
    first_field = jnp.take_along_axis(field_pool, first_slot, axis=1)
    second_field = jnp.take_along_axis(field_pool, second_slot, axis=1)
    return jnp.stack([first_field, second_field], axis=-1).reshape(PAIRS, 2).astype(jnp.int32)


def set_ends(entries, key, least, high):
    longest = entries.shape.index(max(entries.shape))
    spots = []
    for shift in (0, 1):
        where = [jax.random.randint(jax.random.fold_in(key, axis), (), 0, length) for axis, length in enumerate(entries.shape)]
        where[longest] = (where[longest] + shift) % entries.shape[longest]
        spots.append(tuple(where))
    return entries.at[spots[0]].set(least).at[spots[1]].set(high)


def block_levels(key, shape, split, smallest, largest):
    level, own = 1.0, jax.random.fold_in(key, 6)
    for axis_at, shards_of in split:
        steps = jnp.exp(jax.random.uniform(jax.random.fold_in(own, axis_at), (shards_of,), jnp.float32, smallest / len(split), largest / len(split)))
        level = level * jnp.repeat(steps, shape[axis_at] // shards_of).reshape([-1 if axis == axis_at else 1 for axis in range(len(shape))])
    return level


def normal_values(own_key, shape, width, bound, cuts=(), kind=jnp.bfloat16):
    drawn = width * jax.random.normal(own_key, shape, jnp.float32)
    if cuts:
        drawn = drawn * block_levels(own_key, shape, cuts, -0.22, 0.18)
    return jnp.clip(drawn, -bound, bound).astype(kind)


def setup_inputs(seed: int = 0) -> dict:
    streams_of = jax.random.split(jax.random.key(seed), 6)
    embeddings = normal_values(streams_of[0], (FIELDS, SAMPLES, D), 1.0, 6.0, ((0, 8), (1, 4)))
    field_width = draw_field_width(jax.random.fold_in(streams_of[5], 71), 0)
    pair_fields = draw_pair_fields(jax.random.fold_in(streams_of[5], 71), 0)
    pair_mats = normal_values(streams_of[3], (PAIRS, D, D), (D * D * PAIRS // 16) ** -0.5, 0.0048828125, ((0, 8),))
    labels = set_ends((jax.random.randint(streams_of[4], (SAMPLES,), 0, 2) < 1).astype(jnp.int32), jax.random.fold_in(streams_of[4], 1), 0, 1)
    return {"embeddings": embeddings, "field_width": field_width, "pair_fields": pair_fields, "pair_mats": pair_mats, "labels": labels}


def reference(embeddings, field_width, pair_fields, pair_mats, labels):
    column_ids = jnp.arange(D, dtype=jnp.int32)
    width_mask = (column_ids[None, :] < field_width[:, None]).astype(jnp.bfloat16)
    masked = embeddings * width_mask[:, None, :]
    blocks = PAIRS // PAIR_DEV
    groups = SAMPLES // SAMP_DEV
    first_ids = pair_fields[:, 0].reshape(blocks, PAIR_DEV)
    second_ids = pair_fields[:, 1].reshape(blocks, PAIR_DEV)
    block_mats = pair_mats.reshape(blocks, PAIR_DEV, D, D)

    def forward(block_item):
        first_block, second_block, mats_block = block_item
        left_rows = masked[first_block].astype(jnp.float32)
        right_rows = masked[second_block].astype(jnp.float32)
        projected = jnp.einsum('psk,pkl->psl', left_rows, mats_block.astype(jnp.float32))
        return jnp.sum(projected * right_rows, axis=(0, 2))

    logits = jnp.sum(lax.map(forward, (first_ids, second_ids, block_mats)), axis=0)
    grad_out = jax.nn.sigmoid(logits) - labels.astype(jnp.float32)

    def backward(accum_grad, block_item):
        first_block, second_block, mats_block = block_item
        left_rows = masked[first_block].astype(jnp.float32)
        right_rows = masked[second_block].astype(jnp.float32)
        mats_float = mats_block.astype(jnp.float32)
        projected = jnp.einsum('psk,pkl->psl', left_rows, mats_float)
        scaled = (grad_out[None, :, None] * left_rows).astype(jnp.bfloat16)
        scaled_groups = scaled.astype(jnp.float32).reshape(PAIR_DEV, groups, SAMP_DEV, D)
        right_groups = right_rows.reshape(PAIR_DEV, groups, SAMP_DEV, D)
        group_part = jnp.einsum('pgsk,pgsl->pgkl', scaled_groups, right_groups).astype(jnp.bfloat16)
        group_part = lax.optimization_barrier(group_part)
        block_grad = jnp.sum(group_part.astype(jnp.float32), axis=1).astype(jnp.bfloat16)
        toward_left = grad_out[None, :, None] * jnp.einsum('psl,pkl->psk', right_rows, mats_float)
        toward_right = grad_out[None, :, None] * projected
        field_ids = jnp.concatenate([first_block, second_block]).astype(jnp.int32)
        contrib = jnp.concatenate([toward_left, toward_right], axis=0)
        matches = field_ids[:, None] == field_ids[None, :]
        leader = jnp.argmax(matches, axis=1).astype(jnp.int32)
        grouped_sum = jnp.zeros_like(contrib).at[leader].add(contrib)
        rounded = lax.optimization_barrier(grouped_sum.astype(jnp.bfloat16))
        grouped_sum = rounded.astype(jnp.float32)
        is_leader = leader == jnp.arange(2 * PAIR_DEV, dtype=jnp.int32)
        accum_grad = accum_grad.at[field_ids].add(jnp.where(is_leader[:, None, None], grouped_sum, jnp.float32(0.0)))
        return accum_grad, block_grad

    initial = jnp.zeros((FIELDS, SAMPLES, D), jnp.float32)
    accum_grad, mats_out = lax.scan(backward, initial, (first_ids, second_ids, block_mats))
    emb_grad = accum_grad * width_mask[:, None, :].astype(jnp.float32)
    return (logits, mats_out.reshape(PAIRS, D, D), emb_grad)
```

```python
import functools

import jax
import jax.numpy as jnp
from jax import lax
from jax.experimental import pallas as pl
from jax.experimental.pallas import tpu as pltpu
from jax.sharding import PartitionSpec as P

CAP = 3
VMEM = pl.BlockSpec(memory_space=pltpu.VMEM)
SMEM = pl.BlockSpec(memory_space=pltpu.SMEM)
HBM = pl.BlockSpec(memory_space=pl.ANY)
F32 = jnp.float32
BF16 = jnp.bfloat16


def pick_rows_kernel(which_ref, table_ref, *refs):
    *sources, out_ref, sems = refs
    slots = out_ref.shape[0]
    for at, source in enumerate(sources):

        @pl.when(which_ref[0] == at)
        def _(source=source):
            @pl.loop(0, slots)
            def _(j):
                pltpu.make_async_copy(source.at[table_ref[j]], out_ref.at[j], sems.at[j]).start()

    @pl.loop(0, slots)
    def _(j):
        pltpu.make_async_copy(sources[0].at[0], out_ref.at[j], sems.at[j]).wait()


def pick_rows(which, table, sources):
    shape = (table.shape[0],) + sources[0].shape[1:]
    size = shape[0] * shape[1] * shape[2] * 2
    return pl.pallas_call(
        pick_rows_kernel,
        out_shape=jax.ShapeDtypeStruct(shape, BF16),
        in_specs=[SMEM, SMEM] + [HBM] * len(sources),
        out_specs=HBM,
        scratch_shapes=[pltpu.SemaphoreType.DMA((shape[0],))],
        cost_estimate=pl.CostEstimate(flops=0, bytes_accessed=2 * size, transcendentals=0),
    )(which, table, *sources)


def forward_kernel(group, slot_ref, width_ref, rows_ref, mats_ref, part_ref, sums_ref, x_ref, u_ref, acc_ref):
    step = pl.program_id(0)
    slots, samples, width = x_ref.shape

    @pl.when(step == 0)
    def _():
        columns = lax.broadcasted_iota(jnp.int32, (samples, width), 1)

        @pl.loop(0, slots)
        def _(j):
            x_ref[j] = jnp.where(columns < width_ref[j], rows_ref[j], jnp.zeros_like(rows_ref[j]))
            u_ref[j] = jnp.zeros((samples, width), F32)

        acc_ref[...] = jnp.zeros_like(acc_ref)

    for k in range(group):
        p = step * group + k
        a, b = slot_ref[2 * p], slot_ref[2 * p + 1]
        left, right, mat = x_ref[a], x_ref[b], mats_ref[k]
        projected = jnp.dot(left, mat, preferred_element_type=F32)
        back = lax.dot_general(right, mat, (((1,), (1,)), ((), ())), preferred_element_type=F32)
        acc_ref[...] += projected * right.astype(F32)
        u_ref[b] += projected
        u_ref[a] += back

    @pl.when(step == pl.num_programs(0) - 1)
    def _():
        @pl.loop(0, slots)
        def _(j):
            sums_ref[j] = u_ref[j].astype(BF16)

        total = acc_ref[:, 0:128]
        for at in range(128, width, 128):
            total = total + acc_ref[:, at : at + 128]
        part_ref[...] = jnp.sum(total.T, axis=0, keepdims=True)


def forward(slot_index, slot_width, rows, mats, group=4):
    slots, samples, width = rows.shape
    pairs = mats.shape[0]
    whole = lambda *shape: pl.BlockSpec(shape, lambda i: (0,) * len(shape))
    return pl.pallas_call(
        functools.partial(forward_kernel, group),
        grid=(pairs // group,),
        out_shape=(
            jax.ShapeDtypeStruct((1, samples), F32),
            jax.ShapeDtypeStruct(rows.shape, BF16),
        ),
        in_specs=[SMEM, SMEM, whole(*rows.shape), pl.BlockSpec((group, width, width), lambda i: (i, 0, 0))],
        out_specs=(whole(1, samples), whole(*rows.shape)),
        scratch_shapes=[
            pltpu.VMEM(rows.shape, BF16),
            pltpu.VMEM(rows.shape, F32),
            pltpu.VMEM((samples, width), F32),
        ],
        compiler_params=pltpu.CompilerParams(vmem_limit_bytes=60 * 2**20),
        cost_estimate=pl.CostEstimate(
            flops=4 * pairs * samples * width * width, bytes_accessed=2 * pairs * width * width, transcendentals=0
        ),
    )(slot_index, slot_width, rows, mats)


def emb_grad_kernel(table_ref, width_ref, back_ref, grad_ref, out_ref):
    fields, samples, width = out_ref.shape

    @pl.loop(0, fields)
    def _(f):
        out_ref[f] = jnp.zeros((samples, width), F32)

    @pl.loop(0, back_ref.shape[0])
    def _(j):
        f = table_ref[j]
        out_ref[f] += back_ref[j].astype(F32)

    grad = jnp.broadcast_to(grad_ref[...], (128, samples)).T
    grad = jnp.concatenate([grad] * (width // 128), axis=1)
    columns = lax.broadcasted_iota(jnp.int32, (samples, width), 1)

    @pl.loop(0, fields)
    def _(f):
        out_ref[f] = jnp.where(columns < width_ref[f], out_ref[f] * grad, 0.0)


def emb_grad_of(table, own_width, back, grad, fields):
    slots, samples, width = back.shape
    return pl.pallas_call(
        emb_grad_kernel,
        out_shape=jax.ShapeDtypeStruct((fields, samples, width), F32),
        in_specs=[SMEM, SMEM, VMEM, VMEM],
        out_specs=VMEM,
        compiler_params=pltpu.CompilerParams(vmem_limit_bytes=60 * 2**20),
        cost_estimate=pl.CostEstimate(
            flops=slots * samples * width, bytes_accessed=fields * samples * width * 6, transcendentals=0
        ),
    )(table, own_width, back, grad)


def mat_grad_kernel(count, slot_ref, width_ref, source_ref, first_ref, grads_ref, *refs):
    blocks = refs[:count]
    out_ref, x_ref, t_ref, acc_ref, sems = refs[count:]
    _, slots, samples, width = x_ref.shape
    pairs, rows, _ = acc_ref.shape
    columns = lax.broadcasted_iota(jnp.int32, (samples, width), 1)
    own_row = lax.broadcasted_iota(jnp.int32, (rows, width), 0) + first_ref[0]
    pick = (lax.broadcasted_iota(jnp.int32, (rows, width), 1) == own_row).astype(BF16)

    def load(at):
        return pltpu.make_async_copy(blocks[at], x_ref.at[at % 2], sems.at[at % 2])

    load(0).start()
    for at in range(count):
        if at + 1 < count:
            load(at + 1).start()
        load(at).wait()
        now = at % 2
        grad = grads_ref[source_ref[at]]

        @pl.loop(0, slots)
        def _(j):
            x = jnp.where(columns < width_ref[j], x_ref[now, j], jnp.zeros((samples, width), BF16))
            x_ref[now, j] = x
            turned = lax.dot_general(pick, x, (((1,), (1,)), ((), ())), preferred_element_type=F32)
            t_ref[j] = (turned * grad).astype(BF16)

        @pl.loop(0, pairs, unroll=4)
        def _(p):
            a, b = slot_ref[2 * p], slot_ref[2 * p + 1]
            term = jnp.dot(t_ref[a], x_ref[now, b], preferred_element_type=F32)
            if at == 0:
                acc_ref[p] = term
            elif at < count - 1:
                acc_ref[p] += term
            else:
                out_ref[p] = (acc_ref[p] + term).astype(BF16)


def mat_grad_of(slot_index, slot_width, sources, first, grads, blocks, rows):
    slots, samples, width = blocks[0].shape
    pairs = slot_index.shape[0] // 2
    return pl.pallas_call(
        functools.partial(mat_grad_kernel, len(blocks)),
        out_shape=jax.ShapeDtypeStruct((pairs, rows, width), BF16),
        in_specs=[SMEM, SMEM, SMEM, SMEM, VMEM] + [HBM] * len(blocks),
        out_specs=VMEM,
        scratch_shapes=[
            pltpu.VMEM((2, slots, samples, width), BF16),
            pltpu.VMEM((slots, rows, samples), BF16),
            pltpu.VMEM((pairs, rows, width), F32),
            pltpu.SemaphoreType.DMA((2,)),
        ],
        compiler_params=pltpu.CompilerParams(vmem_limit_bytes=60 * 2**20),
        cost_estimate=pl.CostEstimate(
            flops=2 * len(blocks) * pairs * rows * samples * width,
            bytes_accessed=2 * len(blocks) * slots * samples * width,
            transcendentals=0,
        ),
    )(slot_index, slot_width, sources, first, grads, *blocks)


def line_rounds(n):
    order = []
    for i in range(n):
        order.append([(up, k) for k in range(1, n) for up in (True, False) if (i - k >= 0 if up else i + k < n)])
    return order


def shards(embeddings, field_width, pair_fields, pair_mats, labels):
    owners = lax.axis_size("pair")
    groups = lax.axis_size("dp")
    owner = lax.axis_index("pair")
    group = lax.axis_index("dp")
    fields, samples, width = embeddings.shape
    pairs = pair_mats.shape[0]
    every = owners * fields

    pair_list = pair_fields.T
    field_ids = jnp.arange(fields, dtype=jnp.int32)
    slot_ids = jnp.arange(CAP, dtype=jnp.int32)
    local = pair_list.reshape(2, owners, 1, pairs) - owner * fields
    needed = jnp.any(local == field_ids[None, None, :, None], axis=(0, 3)).astype(jnp.int32)
    rank = jnp.sum(jnp.where(field_ids[:, None] > field_ids[None, :], needed[:, None, :], 0), axis=2)
    chosen = (needed[:, None, :] > 0) & (rank[:, None, :] == slot_ids[None, :, None])
    table = jnp.sum(jnp.where(chosen, field_ids[None, None, :], 0), axis=2).reshape(-1)

    mine = lax.dynamic_slice_in_dim(pair_list, owner * pairs, pairs, 1)
    all_ids = jnp.arange(every, dtype=jnp.int32)
    hit = mine.T.reshape(-1)[:, None] == all_ids[None, :]
    wanted = jnp.any(hit, axis=0).astype(jnp.int32).reshape(owners, fields)
    place = jnp.sum(jnp.where(field_ids[:, None] > field_ids[None, :], wanted[:, None, :], 0), axis=2)
    slot_of = jnp.arange(owners, dtype=jnp.int32)[:, None] * CAP + place
    slot_index = jnp.sum(jnp.where(hit, slot_of.reshape(-1)[None, :], 0), axis=1)
    taken = (wanted[:, None, :] > 0) & (place[:, None, :] == slot_ids[None, :, None])
    slot_width = jnp.sum(jnp.where(taken, field_width.reshape(owners, 1, fields), 0), axis=2).reshape(-1)
    own_width = lax.dynamic_slice_in_dim(field_width, owner * fields, fields, 0)

    up, down = [embeddings], [embeddings]
    for k in range(1, groups):
        up.append(lax.ppermute(up[-1], "dp", [(i, i + 1) for i in range(k - 1, groups - 1)]))
        down.append(lax.ppermute(down[-1], "dp", [(i, i - 1) for i in range(1, groups - k + 1)]))

    def exchange(rows):
        return lax.all_to_all(
            rows.reshape(owners, CAP, samples, width), "pair", split_axis=0, concat_axis=0, tiled=True
        ).reshape(owners * CAP, samples, width)

    zero = jnp.zeros((1,), jnp.int32)
    received = exchange(pick_rows(zero, table, [embeddings]))

    part, sums = forward(slot_index, slot_width, received, pair_mats)
    back = exchange(sums)
    note = jnp.concatenate([part, labels.astype(F32)[None, :]], axis=0)
    notes = lax.all_gather(note, ("dp", "pair"), axis=0).reshape(groups, owners, 2, samples)
    every_logit = jnp.sum(notes[:, :, 0], axis=1)
    grads = (jax.nn.sigmoid(every_logit) - notes[:, 0, 1])[:, None, :]
    logits = lax.dynamic_index_in_dim(every_logit, group, 0, keepdims=False)
    own_grad = lax.dynamic_index_in_dim(grads, group, 0, keepdims=False)

    emb_grad = emb_grad_of(table, own_width, back, own_grad, fields)

    order = line_rounds(groups)
    blocks, sources = [received], [group]
    for r in range(groups - 1):
        ways = sorted({order[i][r] for i in range(groups)})
        which = jnp.array([[ways.index(order[i][r])] for i in range(groups)], jnp.int32)
        origin = jnp.array([i - k if u else i + k for i, (u, k) in ((i, order[i][r]) for i in range(groups))], jnp.int32)
        candidates = [(up if u else down)[k] for u, k in ways]
        which = lax.dynamic_index_in_dim(which, group, 0, keepdims=False)
        sources.append(lax.dynamic_index_in_dim(origin, group, 0, keepdims=False))
        blocks.append(exchange(pick_rows(which, table, candidates)))
    rows = width // groups
    mat_grad = mat_grad_of(
        slot_index, slot_width, jnp.stack(sources).astype(jnp.int32), (group * rows).reshape(1), grads, blocks, rows
    )
    return (logits, mat_grad, emb_grad)


def solution(mesh):
    in_specs = (P("pair", "dp", None), P(), P(), P("pair", None, None), P("dp"))
    out_specs = (P("dp"), P("pair", "dp", None), P("pair", "dp", None))
    return jax.shard_map(shards, mesh=mesh, in_specs=in_specs, out_specs=out_specs, check_vma=False)
```

```python
import functools
import math

import jax
import jax.numpy as jnp
from jax import lax
from jax.experimental import pallas as pl
from jax.experimental.pallas import tpu as pltpu
from jax.sharding import PartitionSpec as P

CAP = 3
NOTE = 16
RAW = 64
VMEM = pl.BlockSpec(memory_space=pltpu.VMEM)
SMEM = pl.BlockSpec(memory_space=pltpu.SMEM)
HBM = pl.BlockSpec(memory_space=pl.ANY)
F32 = jnp.float32
BF16 = jnp.bfloat16
CHEAP = pl.CostEstimate(flops=0, bytes_accessed=1 << 20, transcendentals=0)


def limit(size):
    return pltpu.CompilerParams(vmem_limit_bytes=size + (4 << 20))


def pick_rows_kernel(ways, which_ref, table_ref, *refs):
    *sources, out_ref, sems = refs
    slots = out_ref.shape[0]
    lines = sources[0].shape[1]
    for r, choices in enumerate(ways):
        for at, source in enumerate(choices):

            @pl.when(which_ref[r] == at)
            def _(r=r, source=source):
                @pl.loop(0, slots)
                def _(j):
                    place = out_ref.at[j, pl.ds(r * lines, lines), :]
                    pltpu.make_async_copy(sources[source].at[table_ref[j]], place, sems.at[r, j]).start()

    for r in range(len(ways)):

        @pl.loop(0, slots)
        def _(j, r=r):
            place = out_ref.at[j, pl.ds(r * lines, lines), :]
            pltpu.make_async_copy(sources[0].at[0], place, sems.at[r, j]).wait()


def pick_rows(ways, which, table, sources):
    _, lines, width = sources[0].shape
    shape = (table.shape[0], len(ways) * lines, width)
    return pl.pallas_call(
        functools.partial(pick_rows_kernel, ways),
        out_shape=jax.ShapeDtypeStruct(shape, BF16),
        in_specs=[SMEM, SMEM] + [HBM] * len(sources),
        out_specs=VMEM,
        scratch_shapes=[pltpu.SemaphoreType.DMA((len(ways), shape[0]))],
        compiler_params=limit(math.prod(shape) * 2),
        cost_estimate=CHEAP,
    )(which, table, *sources)


def forward_kernel(group, slot_ref, width_ref, rows_ref, mats_ref, sums_ref, x_ref, u_ref, acc_ref):
    step = pl.program_id(0)
    slots, samples, width = x_ref.shape

    @pl.when(step == 0)
    def _():
        columns = lax.broadcasted_iota(jnp.int32, (samples, width), 1)

        @pl.loop(0, slots)
        def _(j):
            x_ref[j] = jnp.where(columns < width_ref[j], rows_ref[j], jnp.zeros_like(rows_ref[j]))
            u_ref[j] = jnp.zeros((samples, width), F32)

        acc_ref[...] = jnp.zeros_like(acc_ref)

    acc = jnp.zeros((samples, width), F32)
    for k in range(group):
        p = step * group + k
        a, b = slot_ref[2 * p], slot_ref[2 * p + 1]
        left, right, mat = x_ref[a], x_ref[b], mats_ref[k]
        projected = jnp.dot(left, mat, preferred_element_type=F32)
        back = lax.dot_general(right, mat, (((1,), (1,)), ((), ())), preferred_element_type=F32)
        acc += projected * right.astype(F32)
        u_ref[b] += projected
        u_ref[a] += back
    acc_ref[...] += acc

    @pl.when(step == pl.num_programs(0) - 1)
    def _():
        total = acc_ref[:, 0:128]
        for at in range(128, width, 128):
            total = total + acc_ref[:, at : at + 128]
        part = jnp.sum(total.T, axis=0, keepdims=True)
        note = jnp.zeros((NOTE, width), F32)
        for row in range(3):
            piece = part.astype(BF16).astype(F32)
            part = part - piece
            at = lax.broadcasted_iota(jnp.int32, (NOTE, width), 0) == row
            note = jnp.where(at, jnp.concatenate([piece] * (width // samples), axis=1), note)
        lines = CAP * samples

        @pl.loop(0, slots // CAP)
        def _(o):
            for c in range(CAP):
                sums_ref[o, c * samples : (c + 1) * samples, :] = u_ref[o * CAP + c].astype(BF16)
            sums_ref[o, lines : lines + NOTE, :] = note.astype(BF16)


def forward(slot_index, slot_width, rows, mats, group=8):
    slots, samples, width = rows.shape
    pairs = mats.shape[0]
    whole = lambda *shape: pl.BlockSpec(shape, lambda i: (0,) * len(shape))
    sums = (slots // CAP, CAP * samples + NOTE, width)
    return pl.pallas_call(
        functools.partial(forward_kernel, group),
        grid=(pairs // group,),
        out_shape=jax.ShapeDtypeStruct(sums, BF16),
        in_specs=[SMEM, SMEM, whole(*rows.shape), pl.BlockSpec((group, width, width), lambda i: (i, 0, 0))],
        out_specs=whole(*sums),
        scratch_shapes=[
            pltpu.VMEM(rows.shape, BF16),
            pltpu.VMEM(rows.shape, F32),
            pltpu.VMEM((samples, width), F32),
        ],
        compiler_params=limit(14 * math.prod(rows.shape) + 4 * group * width * width),
        cost_estimate=CHEAP,
    )(slot_index, slot_width, rows, mats)


def emb_grad_kernel(table_ref, width_ref, back_ref, labels_ref, out_ref, logit_ref, grad_ref):
    fields, samples, width = out_ref.shape
    owners = back_ref.shape[0]
    lines = CAP * samples

    @pl.loop(0, fields)
    def _(f):
        out_ref[f] = jnp.zeros((samples, width), F32)

    @pl.loop(0, owners)
    def _(o):
        for c in range(CAP):
            f = table_ref[o * CAP + c]
            out_ref[f] += back_ref[o, c * samples : (c + 1) * samples, :].astype(F32)

    note = back_ref[0, lines : lines + NOTE, 0:samples].astype(F32)
    for o in range(1, owners):
        note += back_ref[o, lines : lines + NOTE, 0:samples].astype(F32)
    logit = note[0:1] + note[1:2] + note[2:3]
    grad = jax.nn.sigmoid(logit) - labels_ref[...].astype(F32)
    logit_ref[...] = logit
    grad_ref[...] = grad
    factor = jnp.broadcast_to(grad, (128, samples)).T
    factor = jnp.concatenate([factor] * (width // 128), axis=1)
    columns = lax.broadcasted_iota(jnp.int32, (samples, width), 1)

    @pl.loop(0, fields)
    def _(f):
        out_ref[f] = jnp.where(columns < width_ref[f], out_ref[f] * factor, 0.0)


def emb_grad_of(table, own_width, back, labels, fields):
    samples, width = labels.shape[1], back.shape[2]
    return pl.pallas_call(
        emb_grad_kernel,
        out_shape=(
            jax.ShapeDtypeStruct((fields, samples, width), F32),
            jax.ShapeDtypeStruct((1, samples), F32),
            jax.ShapeDtypeStruct((1, samples), F32),
        ),
        in_specs=[SMEM, SMEM, VMEM, VMEM],
        out_specs=(VMEM, VMEM, VMEM),
        compiler_params=limit(math.prod(back.shape) * 2 + fields * samples * width * 4),
        cost_estimate=CHEAP,
    )(table, own_width, back, labels)


def mat_grad_kernel(ways, chunk, slot_ref, width_ref, which_ref, source_ref, first_ref, grads_ref, own_ref, raw_ref, *refs):
    *links, out_ref, x_ref, t_ref, acc_ref, sems = refs
    count = len(ways) + 1
    width = x_ref.shape[2]
    slots, samples, _ = own_ref.shape
    kept_lines = links[0].shape[1]
    raw_lines = samples - kept_lines
    pairs, rows, _ = acc_ref.shape
    own_row = lax.broadcasted_iota(jnp.int32, (rows, width), 0) + first_ref[0]
    columns = lax.broadcasted_iota(jnp.int32, (rows, width), 1)
    pick = (columns == own_row).astype(BF16)

    def place(k, low, size):
        return x_ref.at[:, pl.ds(k * samples + low, size), :]

    for start in range(0, count, chunk):
        waits = []
        for k in range(chunk):
            if start + k == 0:
                waits.append(pltpu.make_async_copy(own_ref, place(k, 0, samples), sems.at[k, 0]))
                waits[-1].start()
                continue
            r = start + k - 1
            raw = raw_ref.at[:, pl.ds(r * raw_lines, raw_lines), :]
            waits.append(pltpu.make_async_copy(raw, place(k, 0, raw_lines), sems.at[k, 0]))
            waits[-1].start()
            for at, link in enumerate(ways[r]):

                @pl.when(which_ref[r] == at)
                def _(k=k, link=link):
                    pltpu.make_async_copy(links[link], place(k, raw_lines, kept_lines), sems.at[k, 1]).start()

            waits.append(pltpu.make_async_copy(links[0], place(k, raw_lines, kept_lines), sems.at[k, 1]))
        for copy in waits:
            copy.wait()
        grad = jnp.concatenate([grads_ref[source_ref[start + k]] for k in range(chunk)], axis=1)

        @pl.loop(0, slots, unroll=4)
        def _(j, grad=grad):
            turned = lax.dot_general(pick, x_ref[j], (((1,), (1,)), ((), ())), preferred_element_type=F32)
            t_ref[j] = (turned * grad).astype(BF16)

        @pl.loop(0, pairs, unroll=4)
        def _(p, start=start):
            a, b = slot_ref[2 * p], slot_ref[2 * p + 1]
            term = jnp.dot(t_ref[a], x_ref[b], preferred_element_type=F32)
            if start > 0:
                term += acc_ref[p]
            if start + chunk < count:
                acc_ref[p] = term
            else:
                kept = (own_row < width_ref[a]) & (columns < width_ref[b])
                out_ref[p] = jnp.where(kept, term, 0.0).astype(BF16)


def mat_grad_of(ways, slot_index, slot_width, which, sources, first, grads, own, raw, links, rows):
    slots, samples, width = own.shape
    pairs = slot_index.shape[0] // 2
    chunk = len(ways) + 1
    while chunk * slots * samples * width > (8 << 20) and chunk % 2 == 0:
        chunk //= 2
    size = chunk * slots * samples * (width + rows) * 2 + pairs * rows * width * 6
    return pl.pallas_call(
        functools.partial(mat_grad_kernel, ways, chunk),
        out_shape=jax.ShapeDtypeStruct((pairs, rows, width), BF16),
        in_specs=[SMEM, SMEM, SMEM, SMEM, SMEM, VMEM] + [HBM] * (2 + len(links)),
        out_specs=VMEM,
        scratch_shapes=[
            pltpu.VMEM((slots, chunk * samples, width), BF16),
            pltpu.VMEM((slots, rows, chunk * samples), BF16),
            pltpu.VMEM((pairs, rows, width), F32),
            pltpu.SemaphoreType.DMA((chunk, 2)),
        ],
        compiler_params=limit(size),
        cost_estimate=CHEAP,
    )(slot_index, slot_width, which, sources, first, grads, own, raw, *links)


def line_rounds(n):
    order = []
    for i in range(n):
        order.append([(up, k) for k in range(1, n) for up in (True, False) if (i - k >= 0 if up else i + k < n)])
    return order


def shards(embeddings, field_width, pair_fields, pair_mats, labels):
    owners = lax.axis_size("pair")
    groups = lax.axis_size("dp")
    owner = lax.axis_index("pair")
    group = lax.axis_index("dp")
    fields, samples, width = embeddings.shape
    pairs = pair_mats.shape[0]
    every = owners * fields

    pair_list = pair_fields.T
    field_ids = jnp.arange(fields, dtype=jnp.int32)
    slot_ids = jnp.arange(CAP, dtype=jnp.int32)
    local = pair_list.reshape(2, owners, 1, pairs) - owner * fields
    needed = jnp.any(local == field_ids[None, None, :, None], axis=(0, 3)).astype(jnp.int32)
    rank = jnp.sum(jnp.where(field_ids[:, None] > field_ids[None, :], needed[:, None, :], 0), axis=2)
    chosen = (needed[:, None, :] > 0) & (rank[:, None, :] == slot_ids[None, :, None])
    table = jnp.sum(jnp.where(chosen, field_ids[None, None, :], 0), axis=2).reshape(-1)

    mine = lax.dynamic_slice_in_dim(pair_list, owner * pairs, pairs, 1)
    all_ids = jnp.arange(every, dtype=jnp.int32)
    hit = mine.T.reshape(-1)[:, None] == all_ids[None, :]
    wanted = jnp.any(hit, axis=0).astype(jnp.int32).reshape(owners, fields)
    place = jnp.sum(jnp.where(field_ids[:, None] > field_ids[None, :], wanted[:, None, :], 0), axis=2)
    slot_of = jnp.arange(owners, dtype=jnp.int32)[:, None] * CAP + place
    slot_index = jnp.sum(jnp.where(hit, slot_of.reshape(-1)[None, :], 0), axis=1)
    taken = (wanted[:, None, :] > 0) & (place[:, None, :] == slot_ids[None, :, None])
    slot_width = jnp.sum(jnp.where(taken, field_width.reshape(owners, 1, fields), 0), axis=2).reshape(-1)
    own_width = lax.dynamic_slice_in_dim(field_width, owner * fields, fields, 0)

    def chain(first):
        up, down = [first], [first]
        for k in range(1, groups):
            up.append(lax.ppermute(up[-1], "dp", [(i, i + 1) for i in range(k - 1, groups - 1)]))
            down.append(lax.ppermute(down[-1], "dp", [(i, i - 1) for i in range(1, groups - k + 1)]))
            yield up[-1], down[-1]

    def exchange(rows):
        lines = rows.reshape(owners, -1, width)
        return lax.all_to_all(lines, "pair", split_axis=0, concat_axis=0, tiled=True)

    tie = lax.optimization_barrier
    order = line_rounds(groups)
    ways, which, origin = [], [], []
    for r in range(groups - 1):
        names = sorted({order[i][r] for i in range(groups)})
        ways.append([2 * (k - 1) + (not up) for up, k in names])
        which.append([names.index(order[i][r]) for i in range(groups)])
        origin.append([i - order[i][r][1] if order[i][r][0] else i + order[i][r][1] for i in range(groups)])
    places = jnp.array([list(w) + [i] + list(s) for i, (w, s) in enumerate(zip(zip(*which), zip(*origin)))], jnp.int32)
    places = lax.dynamic_index_in_dim(places, group, 0, keepdims=False)
    which, sources = places[: groups - 1], places[groups - 1 :]

    raw_steps = chain(embeddings[:, :RAW])
    raw = []
    for _ in range(max(1, groups - 2)):
        raw += next(raw_steps)
    picked = pick_rows([[0]], jnp.zeros((1,), jnp.int32), table, [embeddings])
    received = exchange(picked).reshape(owners * CAP, samples, width)
    received, raw = tie((received, raw))

    for step in raw_steps:
        raw += step
    kept_steps = chain(received[:, RAW:])
    sums = forward(slot_index, slot_width, received, pair_mats)
    sums, raw = tie((sums, raw))
    back = exchange(sums)
    far = pick_rows(ways, which, table, raw)
    kept = [*next(kept_steps)]
    far, kept = tie((far, kept))
    far = exchange(far).reshape(owners * CAP, -1, width)
    for step in kept_steps:
        kept += step
    emb_grad, logits, grad = emb_grad_of(table, own_width, back, labels[None, :], fields)
    logits = logits.reshape(samples)
    grads = lax.all_gather(grad, "dp", axis=0)
    rows = width // groups
    mat_grad = mat_grad_of(
        ways, slot_index, slot_width, which, sources, (group * rows).reshape(1), grads, received, far, kept, rows
    )
    return (logits, mat_grad, emb_grad)


def solution(mesh):
    in_specs = (P("pair", "dp", None), P(), P(), P("pair", None, None), P("dp"))
    out_specs = (P("dp"), P("pair", "dp", None), P("pair", "dp", None))
    return jax.shard_map(shards, mesh=mesh, in_specs=in_specs, out_specs=out_specs, check_vma=False)
```

```python
import functools
import math

import jax
import jax.numpy as jnp
from jax import lax
from jax.experimental import pallas as pl
from jax.experimental.pallas import tpu as pltpu
from jax.sharding import PartitionSpec as P

CAP = 3
NOTE = 16
RAW = 48
VMEM = pl.BlockSpec(memory_space=pltpu.VMEM)
SMEM = pl.BlockSpec(memory_space=pltpu.SMEM)
HBM = pl.BlockSpec(memory_space=pl.ANY)
F32 = jnp.float32
BF16 = jnp.bfloat16
CHEAP = pl.CostEstimate(flops=0, bytes_accessed=0, transcendentals=0)


def limit(size):
    return pltpu.CompilerParams(vmem_limit_bytes=size + (4 << 20))


def own_rows_kernel(owner_ref, pairs_ref, rows_ref, out_ref, near_ref, table_ref, scalar_ref, sems, table_sem):
    fields = rows_ref.shape[0]
    owners = out_ref.shape[0]
    lines, width = out_ref.shape[1] // CAP, out_ref.shape[2]
    total = pairs_ref.shape[1]
    near = pltpu.make_async_copy(rows_ref.at[:, pl.ds(0, near_ref.shape[1]), :], near_ref, sems.at[owners * CAP])
    near.start()
    local = pairs_ref[...] - owner_ref[0] * fields
    field = lax.broadcasted_iota(jnp.int32, (fields, total), 0)
    hit = ((local[0:1] == field) | (local[1:2] == field)).astype(BF16)
    low = lax.broadcasted_iota(jnp.int32, (total, 128), 1) * (total // owners)
    at = lax.broadcasted_iota(jnp.int32, (total, 128), 0)
    segment = ((at >= low) & (at < low + total // owners)).astype(BF16)
    needed = jnp.dot(hit, segment, preferred_element_type=F32) > 0
    before = lax.broadcasted_iota(jnp.int32, (fields, fields), 0) > lax.broadcasted_iota(jnp.int32, (fields, fields), 1)
    rank = jnp.dot(before.astype(BF16), needed.astype(BF16), preferred_element_type=F32)
    ids = lax.broadcasted_iota(jnp.int32, (fields, 128), 0).astype(F32)
    rows = lax.broadcasted_iota(jnp.int32, (8, 128), 0)
    table = jnp.zeros((8, 128), F32)
    for c in range(CAP):
        chosen = jnp.sum(jnp.where(needed & (rank == c), ids, 0.0), axis=0, keepdims=True)
        table = jnp.where(rows == c, chosen, table)
    table_ref[...] = table.astype(jnp.int32)
    copy = pltpu.make_async_copy(table_ref, scalar_ref, table_sem)
    copy.start()
    copy.wait()

    def move(d, c, f):
        place = out_ref.at[d, pl.ds(c * lines, lines), :]
        return pltpu.make_async_copy(rows_ref.at[f], place, sems.at[d * CAP + c])

    @pl.loop(0, owners)
    def _(d):
        for c in range(CAP):
            move(d, c, scalar_ref[c, d]).start()

    @pl.loop(0, owners)
    def _(d):
        for c in range(CAP):
            move(d, c, 0).wait()

    near.wait()


def own_rows(owner, pair_list, embeddings, owners):
    fields, samples, width = embeddings.shape
    out = (owners, CAP * samples, width)
    near = (fields, RAW, width)
    return pl.pallas_call(
        own_rows_kernel,
        out_shape=(
            jax.ShapeDtypeStruct(out, BF16),
            jax.ShapeDtypeStruct(near, BF16),
            jax.ShapeDtypeStruct((8, 128), jnp.int32),
        ),
        in_specs=[SMEM, VMEM, HBM],
        out_specs=(VMEM, VMEM, VMEM),
        scratch_shapes=[
            pltpu.SMEM((8, 128), jnp.int32),
            pltpu.SemaphoreType.DMA((owners * CAP + 1,)),
            pltpu.SemaphoreType.DMA,
        ],
        compiler_params=limit(56 << 20),
        cost_estimate=CHEAP,
    )(owner, pair_list, embeddings)


def far_rows_kernel(ways, count, owner_ref, which_ref, table_ref, *refs):
    sources, outs, sems = refs[:count], refs[count:-1], refs[-1]
    lines = sources[0].shape[1]

    def move(r, source, k, c, f):
        place = outs[k].at[c, pl.ds(r * lines, lines), :]
        return pltpu.make_async_copy(source.at[f], place, sems.at[r, k * CAP + c])

    for r, choices in enumerate(ways):
        for at, source in enumerate(choices):

            @pl.when(which_ref[r] == at)
            def _(r=r, source=source):
                for k in range(len(outs)):
                    for c in range(CAP):
                        move(r, sources[source], k, c, table_ref[c, owner_ref[0] ^ k]).start()

    for r in range(len(ways)):
        for k in range(len(outs)):
            for c in range(CAP):
                move(r, sources[0], k, c, 0).wait()


def far_rows(ways, owner, which, table, sources, owners):
    _, lines, width = sources[0].shape
    shape = (CAP, len(ways) * lines, width)
    return pl.pallas_call(
        functools.partial(far_rows_kernel, ways, len(sources)),
        out_shape=[jax.ShapeDtypeStruct(shape, BF16)] * owners,
        in_specs=[SMEM, SMEM, SMEM] + [HBM] * len(sources),
        out_specs=[VMEM] * owners,
        scratch_shapes=[pltpu.SemaphoreType.DMA((len(ways), owners * CAP))],
        compiler_params=limit(owners * math.prod(shape) * 2),
        cost_estimate=CHEAP,
    )(owner, which, table, *sources)


def forward_kernel(group, slot_ref, width_ref, rows_ref, mats_ref, sums_ref, x_ref, u_ref, acc_ref):
    step = pl.program_id(0)
    slots, samples, width = x_ref.shape

    @pl.when(step == 0)
    def _():
        columns = lax.broadcasted_iota(jnp.int32, (samples, width), 1)

        @pl.loop(0, slots)
        def _(j):
            x_ref[j] = jnp.where(columns < width_ref[j], rows_ref[j], jnp.zeros_like(rows_ref[j]))
            u_ref[j] = jnp.zeros((samples, width), F32)

        acc_ref[...] = jnp.zeros_like(acc_ref)

    acc = jnp.zeros((samples, width), F32)
    for k in range(group):
        p = step * group + k
        a, b = slot_ref[2 * p], slot_ref[2 * p + 1]
        left, right, mat = x_ref[a], x_ref[b], mats_ref[k]
        projected = jnp.dot(left, mat, preferred_element_type=F32)
        back = lax.dot_general(right, mat, (((1,), (1,)), ((), ())), preferred_element_type=F32)
        acc += projected * right.astype(F32)
        u_ref[b] += projected
        u_ref[a] += back
    acc_ref[...] += acc

    @pl.when(step == pl.num_programs(0) - 1)
    def _():
        total = acc_ref[:, 0:128]
        for at in range(128, width, 128):
            total = total + acc_ref[:, at : at + 128]
        part = jnp.sum(total.T, axis=0, keepdims=True)
        note = jnp.zeros((NOTE, width), F32)
        for row in range(3):
            piece = part.astype(BF16).astype(F32)
            part = part - piece
            at = lax.broadcasted_iota(jnp.int32, (NOTE, width), 0) == row
            note = jnp.where(at, jnp.concatenate([piece] * (width // samples), axis=1), note)
        lines = CAP * samples

        @pl.loop(0, slots // CAP)
        def _(o):
            for c in range(CAP):
                sums_ref[o, c * samples : (c + 1) * samples, :] = u_ref[o * CAP + c].astype(BF16)
            sums_ref[o, lines : lines + NOTE, :] = note.astype(BF16)


def forward(slot_index, slot_width, rows, mats, group=8):
    slots, samples, width = rows.shape
    pairs = mats.shape[0]
    whole = lambda *shape: pl.BlockSpec(shape, lambda i: (0,) * len(shape))
    sums = (slots // CAP, CAP * samples + NOTE, width)
    return pl.pallas_call(
        functools.partial(forward_kernel, group),
        grid=(pairs // group,),
        out_shape=jax.ShapeDtypeStruct(sums, BF16),
        in_specs=[SMEM, SMEM, whole(*rows.shape), pl.BlockSpec((group, width, width), lambda i: (i, 0, 0))],
        out_specs=whole(*sums),
        scratch_shapes=[
            pltpu.VMEM(rows.shape, BF16),
            pltpu.VMEM(rows.shape, F32),
            pltpu.VMEM((samples, width), F32),
        ],
        compiler_params=limit(14 * math.prod(rows.shape) + 4 * group * width * width),
        cost_estimate=CHEAP,
    )(slot_index, slot_width, rows, mats)


def emb_grad_kernel(table_ref, width_ref, back_ref, labels_ref, out_ref, logit_ref, grad_ref):
    fields, samples, width = out_ref.shape
    owners = back_ref.shape[0]
    lines = CAP * samples

    @pl.loop(0, fields)
    def _(f):
        out_ref[f] = jnp.zeros((samples, width), F32)

    @pl.loop(0, owners)
    def _(o):
        for c in range(CAP):
            f = table_ref[c, o]
            out_ref[f] += back_ref[o, c * samples : (c + 1) * samples, :].astype(F32)

    note = back_ref[0, lines : lines + NOTE, 0:samples].astype(F32)
    for o in range(1, owners):
        note += back_ref[o, lines : lines + NOTE, 0:samples].astype(F32)
    logit = note[0:1] + note[1:2] + note[2:3]
    grad = jax.nn.sigmoid(logit) - labels_ref[...].astype(F32)
    logit_ref[...] = logit
    grad_ref[...] = grad
    factor = jnp.broadcast_to(grad, (128, samples)).T
    factor = jnp.concatenate([factor] * (width // 128), axis=1)
    columns = lax.broadcasted_iota(jnp.int32, (samples, width), 1)

    @pl.loop(0, fields)
    def _(f):
        out_ref[f] = jnp.where(columns < width_ref[f], out_ref[f] * factor, 0.0)


def emb_grad_of(table, own_width, back, labels, fields):
    samples, width = labels.shape[1], back.shape[2]
    return pl.pallas_call(
        emb_grad_kernel,
        out_shape=(
            jax.ShapeDtypeStruct((fields, samples, width), F32),
            jax.ShapeDtypeStruct((1, samples), F32),
            jax.ShapeDtypeStruct((1, samples), F32),
        ),
        in_specs=[SMEM, SMEM, VMEM, VMEM],
        out_specs=(VMEM, VMEM, VMEM),
        compiler_params=limit(math.prod(back.shape) * 2 + fields * samples * width * 4),
        cost_estimate=CHEAP,
    )(table, own_width, back, labels)


def mat_grad_kernel(ways, chunk, owners, slot_ref, width_ref, which_ref, source_ref, first_ref, owner_ref, grads_ref, own_ref, *refs):
    raws = refs[:owners]
    *links, out_ref, x_ref, t_ref, acc_ref, sems = refs[owners:]
    count = len(ways) + 1
    width = x_ref.shape[2]
    slots, samples, _ = own_ref.shape
    kept_lines = links[0].shape[1]
    raw_lines = samples - kept_lines
    pairs, rows, _ = acc_ref.shape
    own_row = lax.broadcasted_iota(jnp.int32, (rows, width), 0) + first_ref[0]
    columns = lax.broadcasted_iota(jnp.int32, (rows, width), 1)
    pick = (columns == own_row).astype(BF16)

    def place(k, low, size):
        return x_ref.at[:, pl.ds(k * samples + low, size), :]

    for start in range(0, count, chunk):
        waits = []
        for k in range(chunk):
            if start + k == 0:
                waits.append(pltpu.make_async_copy(own_ref, place(k, 0, samples), sems.at[k, 0]))
                waits[-1].start()
                continue
            r = start + k - 1
            for d in range(owners):
                raw = raws[d].at[:, pl.ds(r * raw_lines, raw_lines), :]
                spot = x_ref.at[pl.ds((owner_ref[0] ^ d) * CAP, CAP), pl.ds(k * samples, raw_lines), :]
                waits.append(pltpu.make_async_copy(raw, spot, sems.at[k, 2 + d]))
                waits[-1].start()
            for at, link in enumerate(ways[r]):

                @pl.when(which_ref[r] == at)
                def _(k=k, link=link):
                    pltpu.make_async_copy(links[link], place(k, raw_lines, kept_lines), sems.at[k, 1]).start()

            waits.append(pltpu.make_async_copy(links[0], place(k, raw_lines, kept_lines), sems.at[k, 1]))
        for copy in waits:
            copy.wait()
        grad = jnp.concatenate([grads_ref[source_ref[start + k]] for k in range(chunk)], axis=1)

        @pl.loop(0, slots, unroll=4)
        def _(j, grad=grad):
            turned = lax.dot_general(pick, x_ref[j], (((1,), (1,)), ((), ())), preferred_element_type=F32)
            t_ref[j] = (turned * grad).astype(BF16)

        @pl.loop(0, pairs, unroll=4)
        def _(p, start=start):
            a, b = slot_ref[2 * p], slot_ref[2 * p + 1]
            term = jnp.dot(t_ref[a], x_ref[b], preferred_element_type=F32)
            if start > 0:
                term += acc_ref[p]
            if start + chunk < count:
                acc_ref[p] = term
            else:
                kept = (own_row < width_ref[a]) & (columns < width_ref[b])
                out_ref[p] = jnp.where(kept, term, 0.0).astype(BF16)


def mat_grad_of(ways, slot_index, slot_width, which, sources, first, owner, grads, own, raw, links, rows):
    slots, samples, width = own.shape
    pairs = slot_index.shape[0] // 2
    chunk = len(ways) + 1
    while chunk * slots * samples * width > (8 << 20) and chunk % 2 == 0:
        chunk //= 2
    size = chunk * slots * samples * (width + rows) * 2 + pairs * rows * width * 6
    return pl.pallas_call(
        functools.partial(mat_grad_kernel, ways, chunk, len(raw)),
        out_shape=jax.ShapeDtypeStruct((pairs, rows, width), BF16),
        in_specs=[SMEM] * 6 + [VMEM] + [HBM] * (1 + len(raw) + len(links)),
        out_specs=VMEM,
        scratch_shapes=[
            pltpu.VMEM((slots, chunk * samples, width), BF16),
            pltpu.VMEM((slots, rows, chunk * samples), BF16),
            pltpu.VMEM((pairs, rows, width), F32),
            pltpu.SemaphoreType.DMA((chunk, 2 + len(raw))),
        ],
        compiler_params=limit(size),
        cost_estimate=CHEAP,
    )(slot_index, slot_width, which, sources, first, owner, grads, own, *raw, *links)


def line_rounds(n):
    order = []
    for i in range(n):
        order.append([(up, k) for k in range(1, n) for up in (True, False) if (i - k >= 0 if up else i + k < n)])
    return order


def shards(embeddings, field_width, pair_fields, pair_mats, labels):
    owners = lax.axis_size("pair")
    groups = lax.axis_size("dp")
    owner = lax.axis_index("pair")
    group = lax.axis_index("dp")
    fields, samples, width = embeddings.shape
    pairs = pair_mats.shape[0]
    every = owners * fields

    pair_list = pair_fields.T
    field_ids = jnp.arange(fields, dtype=jnp.int32)
    slot_ids = jnp.arange(CAP, dtype=jnp.int32)
    picked, near, table = own_rows(owner.reshape(1), pair_list, embeddings, owners)

    mine = lax.dynamic_slice_in_dim(pair_list, owner * pairs, pairs, 1)
    all_ids = jnp.arange(every, dtype=jnp.int32)
    hit = mine.T.reshape(-1)[:, None] == all_ids[None, :]
    wanted = jnp.any(hit, axis=0).astype(jnp.int32).reshape(owners, fields)
    place = jnp.sum(jnp.where(field_ids[:, None] > field_ids[None, :], wanted[:, None, :], 0), axis=2)
    slot_of = jnp.arange(owners, dtype=jnp.int32)[:, None] * CAP + place
    slot_index = jnp.sum(jnp.where(hit, slot_of.reshape(-1)[None, :], 0), axis=1)
    taken = (wanted[:, None, :] > 0) & (place[:, None, :] == slot_ids[None, :, None])
    slot_width = jnp.sum(jnp.where(taken, field_width.reshape(owners, 1, fields), 0), axis=2).reshape(-1)
    own_width = lax.dynamic_slice_in_dim(field_width, owner * fields, fields, 0)

    def chain(own):
        up = lax.ppermute(own, "dp", [(i, i + 1) for i in range(groups - 1)])
        down = lax.ppermute(own, "dp", [(i + 1, i) for i in range(groups - 1)])
        yield [up, down]
        found = [up, down]
        for k in range(2, groups):
            if k == 2:
                found.append(lax.ppermute(up, "dp", [(i, i + 1) for i in range(1, groups - 1)]))
                found.append(lax.ppermute(down, "dp", [(i, i - 1) for i in range(1, groups - 1)]))
            elif 2 * k >= groups:
                ends = [(i, i + k) for i in range(groups - k)]
                found += [lax.ppermute(own, "dp", ends + [(j, i) for i, j in ends])] * 2
            else:
                found.append(lax.ppermute(own, "dp", [(i, i + k) for i in range(groups - k)]))
                found.append(lax.ppermute(own, "dp", [(i + k, i) for i in range(groups - k)]))
        yield found

    def exchange(rows):
        lines = rows.reshape(owners, -1, width)
        return lax.all_to_all(lines, "pair", split_axis=0, concat_axis=0, tiled=True)

    tie = lax.optimization_barrier
    order = line_rounds(groups)
    ways, which, origin = [], [], []
    for r in range(groups - 1):
        names = sorted({order[i][r] for i in range(groups)})
        ways.append([2 * (k - 1) + (not up) for up, k in names])
        which.append([names.index(order[i][r]) for i in range(groups)])
        origin.append([i - order[i][r][1] if order[i][r][0] else i + order[i][r][1] for i in range(groups)])
    places = jnp.array([list(w) + [i] + list(s) for i, (w, s) in enumerate(zip(zip(*which), zip(*origin)))], jnp.int32)
    places = lax.dynamic_index_in_dim(places, group, 0, keepdims=False)
    which, sources = places[: groups - 1], places[groups - 1 :]

    raw_steps = chain(near)
    close = next(raw_steps)
    received = exchange(picked).reshape(owners * CAP, samples, width)
    received, close[:] = tie((received, close))
    raw = next(raw_steps)
    kept_steps = chain(received[:, RAW:])
    sums = forward(slot_index, slot_width, received, pair_mats)
    sums, raw = tie((sums, raw))
    back = exchange(sums)
    near_kept = next(kept_steps)
    raw, near_kept[:] = tie((raw, near_kept))
    far = far_rows(ways, owner.reshape(1), which, table, raw, owners)
    far = [lax.ppermute(x, "pair", [(i, i ^ k) for i in range(owners)]) if k else x for k, x in enumerate(far)]
    kept = next(kept_steps)
    emb_grad, logits, grad = emb_grad_of(table, own_width, back, labels[None, :], fields)
    logits = logits.reshape(samples)
    grads = lax.all_to_all(jnp.broadcast_to(grad, (groups, 1, samples)), "dp", split_axis=0, concat_axis=0, tiled=True)
    rows = width // groups
    mat_grad = mat_grad_of(
        ways, slot_index, slot_width, which, sources, (group * rows).reshape(1), owner.reshape(1), grads, received, far, kept, rows
    )
    return (logits, mat_grad, emb_grad)


def solution(mesh):
    in_specs = (P("pair", "dp", None), P(), P(), P("pair", None, None), P("dp"))
    out_specs = (P("dp"), P("pair", "dp", None), P("pair", "dp", None))
    return jax.shard_map(shards, mesh=mesh, in_specs=in_specs, out_specs=out_specs, check_vma=False)
```

```python
import functools
import math

import jax
import jax.numpy as jnp
from jax import lax
from jax.experimental import pallas as pl
from jax.experimental.pallas import tpu as pltpu
from jax.sharding import PartitionSpec as P

CAP = 3
NOTE = 16
RAW = 48
VMEM = pl.BlockSpec(memory_space=pltpu.VMEM)
SMEM = pl.BlockSpec(memory_space=pltpu.SMEM)
HBM = pl.BlockSpec(memory_space=pl.ANY)
F32 = jnp.float32
BF16 = jnp.bfloat16
CHEAP = pl.CostEstimate(flops=0, bytes_accessed=0, transcendentals=0)


def limit(size):
    return pltpu.CompilerParams(vmem_limit_bytes=size + (4 << 20))


def own_rows_kernel(owner_ref, pairs_ref, rows_ref, out_ref, near_ref, table_ref, scalar_ref, sems, table_sem):
    fields = rows_ref.shape[0]
    owners = out_ref.shape[0]
    lines, width = out_ref.shape[1] // CAP, out_ref.shape[2]
    total = pairs_ref.shape[1]
    near = pltpu.make_async_copy(rows_ref.at[:, pl.ds(0, near_ref.shape[1]), :], near_ref, sems.at[owners * CAP])
    near.start()
    local = pairs_ref[...] - owner_ref[0] * fields
    field = lax.broadcasted_iota(jnp.int32, (fields, total), 0)
    hit = ((local[0:1] == field) | (local[1:2] == field)).astype(BF16)
    low = lax.broadcasted_iota(jnp.int32, (total, 128), 1) * (total // owners)
    at = lax.broadcasted_iota(jnp.int32, (total, 128), 0)
    segment = ((at >= low) & (at < low + total // owners)).astype(BF16)
    needed = jnp.dot(hit, segment, preferred_element_type=F32) > 0
    before = lax.broadcasted_iota(jnp.int32, (fields, fields), 0) > lax.broadcasted_iota(jnp.int32, (fields, fields), 1)
    rank = jnp.dot(before.astype(BF16), needed.astype(BF16), preferred_element_type=F32)
    ids = lax.broadcasted_iota(jnp.int32, (fields, 128), 0).astype(F32)
    rows = lax.broadcasted_iota(jnp.int32, (8, 128), 0)
    table = jnp.zeros((8, 128), F32)
    for c in range(CAP):
        chosen = jnp.sum(jnp.where(needed & (rank == c), ids, 0.0), axis=0, keepdims=True)
        table = jnp.where(rows == c, chosen, table)
    table_ref[...] = table.astype(jnp.int32)
    copy = pltpu.make_async_copy(table_ref, scalar_ref, table_sem)
    copy.start()
    copy.wait()

    def move(d, c, f):
        place = out_ref.at[d, pl.ds(c * lines, lines), :]
        return pltpu.make_async_copy(rows_ref.at[f], place, sems.at[d * CAP + c])

    @pl.loop(0, owners)
    def _(d):
        for c in range(CAP):
            move(d, c, scalar_ref[c, d]).start()

    @pl.loop(0, owners)
    def _(d):
        for c in range(CAP):
            move(d, c, 0).wait()

    near.wait()


def own_rows(owner, pair_list, embeddings, owners):
    fields, samples, width = embeddings.shape
    out = (owners, CAP * samples, width)
    near = (fields, RAW, width)
    return pl.pallas_call(
        own_rows_kernel,
        out_shape=(
            jax.ShapeDtypeStruct(out, BF16),
            jax.ShapeDtypeStruct(near, BF16),
            jax.ShapeDtypeStruct((8, 128), jnp.int32),
        ),
        in_specs=[SMEM, VMEM, HBM],
        out_specs=(VMEM, VMEM, VMEM),
        scratch_shapes=[
            pltpu.SMEM((8, 128), jnp.int32),
            pltpu.SemaphoreType.DMA((owners * CAP + 1,)),
            pltpu.SemaphoreType.DMA,
        ],
        compiler_params=limit(56 << 20),
        cost_estimate=CHEAP,
    )(owner, pair_list, embeddings)


def far_rows_kernel(ways, count, owner_ref, which_ref, table_ref, *refs):
    sources, outs, sems = refs[:count], refs[count:-1], refs[-1]
    lines = sources[0].shape[1]

    def move(r, source, k, c, f):
        place = outs[k].at[c, pl.ds(r * lines, lines), :]
        return pltpu.make_async_copy(source.at[f], place, sems.at[r, k * CAP + c])

    for r, choices in enumerate(ways):
        for at, source in enumerate(choices):

            @pl.when(which_ref[r] == at)
            def _(r=r, source=source):
                for k in range(len(outs)):
                    for c in range(CAP):
                        move(r, sources[source], k, c, table_ref[c, owner_ref[0] ^ k]).start()

    for r in range(len(ways)):
        for k in range(len(outs)):
            for c in range(CAP):
                move(r, sources[0], k, c, 0).wait()


def far_rows(ways, owner, which, table, sources, owners):
    _, lines, width = sources[0].shape
    shape = (CAP, len(ways) * lines, width)
    return pl.pallas_call(
        functools.partial(far_rows_kernel, ways, len(sources)),
        out_shape=[jax.ShapeDtypeStruct(shape, BF16)] * owners,
        in_specs=[SMEM, SMEM, SMEM] + [HBM] * len(sources),
        out_specs=[VMEM] * owners,
        scratch_shapes=[pltpu.SemaphoreType.DMA((len(ways), owners * CAP))],
        compiler_params=limit(56 << 20),
        cost_estimate=CHEAP,
    )(owner, which, table, *sources)


def forward_kernel(group, slot_ref, width_ref, rows_ref, mats_ref, sums_ref, x_ref, u_ref, acc_ref, mats, sems):
    slots, samples, width = x_ref.shape
    steps = mats.shape[0] // group

    def load(i):
        part = pl.ds(i * group, group)
        return pltpu.make_async_copy(mats_ref.at[part], mats.at[part], sems.at[i])

    for i in range(steps):
        load(i).start()
    columns = lax.broadcasted_iota(jnp.int32, (samples, width), 1)

    @pl.loop(0, slots, unroll=4)
    def _(j):
        x_ref[j] = jnp.where(columns < width_ref[j], rows_ref[j], jnp.zeros_like(rows_ref[j]))
        u_ref[j] = jnp.zeros((samples, width), F32)

    acc_ref[...] = jnp.zeros_like(acc_ref)

    @pl.loop(0, steps)
    def _(i):
        load(i).wait()
        acc = jnp.zeros((samples, width), F32)
        for k in range(group):
            p = i * group + k
            a, b = slot_ref[2 * p], slot_ref[2 * p + 1]
            left, right, mat = x_ref[a], x_ref[b], mats[p]
            projected = jnp.dot(left, mat, preferred_element_type=F32)
            back = lax.dot_general(right, mat, (((1,), (1,)), ((), ())), preferred_element_type=F32)
            acc += projected * right.astype(F32)
            u_ref[b] += projected
            u_ref[a] += back
        acc_ref[...] += acc

    total = acc_ref[:, 0:128]
    for at in range(128, width, 128):
        total = total + acc_ref[:, at : at + 128]
    part = jnp.sum(total.T, axis=0, keepdims=True)
    note = jnp.zeros((NOTE, width), F32)
    for row in range(3):
        piece = part.astype(BF16).astype(F32)
        part = part - piece
        at = lax.broadcasted_iota(jnp.int32, (NOTE, width), 0) == row
        note = jnp.where(at, jnp.concatenate([piece] * (width // samples), axis=1), note)
    lines = CAP * samples

    @pl.loop(0, slots // CAP)
    def _(o):
        for c in range(CAP):
            sums_ref[o, c * samples : (c + 1) * samples, :] = u_ref[o * CAP + c].astype(BF16)
        sums_ref[o, lines : lines + NOTE, :] = note.astype(BF16)


def forward(slot_index, slot_width, rows, mats, group=8):
    slots, samples, width = rows.shape
    sums = (slots // CAP, CAP * samples + NOTE, width)
    return pl.pallas_call(
        functools.partial(forward_kernel, group),
        out_shape=jax.ShapeDtypeStruct(sums, BF16),
        in_specs=[SMEM, SMEM, VMEM, HBM],
        out_specs=VMEM,
        scratch_shapes=[
            pltpu.VMEM(rows.shape, BF16),
            pltpu.VMEM(rows.shape, F32),
            pltpu.VMEM((samples, width), F32),
            pltpu.VMEM(mats.shape, BF16),
            pltpu.SemaphoreType.DMA((mats.shape[0] // group,)),
        ],
        compiler_params=limit(52 << 20),
        cost_estimate=CHEAP,
    )(slot_index, slot_width, rows, mats)


def emb_grad_kernel(table_ref, width_ref, back_ref, labels_ref, out_ref, logit_ref, grad_ref):
    fields, samples, width = out_ref.shape
    owners = back_ref.shape[0]
    lines = CAP * samples

    @pl.loop(0, fields)
    def _(f):
        out_ref[f] = jnp.zeros((samples, width), F32)

    @pl.loop(0, owners)
    def _(o):
        for c in range(CAP):
            f = table_ref[c, o]
            out_ref[f] += back_ref[o, c * samples : (c + 1) * samples, :].astype(F32)

    note = back_ref[0, lines : lines + NOTE, 0:samples].astype(F32)
    for o in range(1, owners):
        note += back_ref[o, lines : lines + NOTE, 0:samples].astype(F32)
    logit = note[0:1] + note[1:2] + note[2:3]
    grad = jax.nn.sigmoid(logit) - labels_ref[...].astype(F32)
    logit_ref[...] = logit
    grad_ref[...] = grad
    factor = jnp.broadcast_to(grad, (128, samples)).T
    factor = jnp.concatenate([factor] * (width // 128), axis=1)
    columns = lax.broadcasted_iota(jnp.int32, (samples, width), 1)

    @pl.loop(0, fields)
    def _(f):
        out_ref[f] = jnp.where(columns < width_ref[f], out_ref[f] * factor, 0.0)


def emb_grad_of(table, own_width, back, labels, fields):
    samples, width = labels.shape[1], back.shape[2]
    return pl.pallas_call(
        emb_grad_kernel,
        out_shape=(
            jax.ShapeDtypeStruct((fields, samples, width), F32),
            jax.ShapeDtypeStruct((1, samples), F32),
            jax.ShapeDtypeStruct((1, samples), F32),
        ),
        in_specs=[SMEM, SMEM, VMEM, VMEM],
        out_specs=(VMEM, VMEM, VMEM),
        compiler_params=limit(math.prod(back.shape) * 2 + fields * samples * width * 4),
        cost_estimate=CHEAP,
    )(table, own_width, back, labels)


def mat_grad_kernel(ways, chunk, owners, slot_ref, width_ref, which_ref, source_ref, first_ref, owner_ref, grads_ref, own_ref, *refs):
    raws = refs[:owners]
    *links, out_ref, x_ref, t_ref, acc_ref, done_ref, sems, done_sems = refs[owners:]
    group = done_ref.shape[0] // done_sems.shape[0]
    count = len(ways) + 1
    width = x_ref.shape[2]
    slots, samples, _ = own_ref.shape
    kept_lines = links[0].shape[1]
    raw_lines = samples - kept_lines
    pairs, rows, _ = acc_ref.shape
    own_row = lax.broadcasted_iota(jnp.int32, (rows, width), 0) + first_ref[0]
    columns = lax.broadcasted_iota(jnp.int32, (rows, width), 1)
    pick = (columns == own_row).astype(BF16)

    def place(k, low, size):
        return x_ref.at[:, pl.ds(k * samples + low, size), :]

    def store(i):
        part = pl.ds(i * group, group)
        return pltpu.make_async_copy(done_ref.at[part], out_ref.at[part], done_sems.at[i])

    for start in range(0, count, chunk):
        waits = [[] for _ in range(chunk)]
        for k in range(chunk):
            if start + k == 0:
                waits[k].append(pltpu.make_async_copy(own_ref, place(k, 0, samples), sems.at[k, 0]))
                waits[k][-1].start()
                continue
            r = start + k - 1
            for d in range(owners):
                raw = raws[d].at[:, pl.ds(r * raw_lines, raw_lines), :]
                spot = x_ref.at[pl.ds((owner_ref[0] ^ d) * CAP, CAP), pl.ds(k * samples, raw_lines), :]
                waits[k].append(pltpu.make_async_copy(raw, spot, sems.at[k, 2 + d]))
                waits[k][-1].start()
            for at, link in enumerate(ways[r]):

                @pl.when(which_ref[r] == at)
                def _(k=k, link=link):
                    pltpu.make_async_copy(links[link], place(k, raw_lines, kept_lines), sems.at[k, 1]).start()

            waits[k].append(pltpu.make_async_copy(links[0], place(k, raw_lines, kept_lines), sems.at[k, 1]))
        for k in range(chunk):
            for copy in waits[k]:
                copy.wait()
            grad = grads_ref[source_ref[start + k]]

            @pl.loop(0, slots, unroll=12)
            def _(j, k=k, grad=grad):
                x = x_ref[j, k * samples : (k + 1) * samples, :]
                turned = lax.dot_general(pick, x, (((1,), (1,)), ((), ())), preferred_element_type=F32)
                t_ref[j, :, k * samples : (k + 1) * samples] = (turned * grad).astype(BF16)

        def term_of(p):
            a, b = slot_ref[2 * p], slot_ref[2 * p + 1]
            term = jnp.dot(t_ref[a], x_ref[b], preferred_element_type=F32)
            return term if start == 0 else term + acc_ref[p]

        if start + chunk < count:

            @pl.loop(0, pairs, unroll=8)
            def _(p, term_of=term_of):
                acc_ref[p] = term_of(p)

            continue

        @pl.loop(0, pairs // group)
        def _(i, term_of=term_of):
            for k in range(group):
                p = i * group + k
                a, b = slot_ref[2 * p], slot_ref[2 * p + 1]
                kept = (own_row < width_ref[a]) & (columns < width_ref[b])
                done_ref[p] = jnp.where(kept, term_of(p), 0.0).astype(BF16)
            store(i).start()

        @pl.loop(0, pairs // group)
        def _(i):
            store(i).wait()


def mat_grad_of(ways, slot_index, slot_width, which, sources, first, owner, grads, own, raw, links, rows):
    slots, samples, width = own.shape
    pairs = slot_index.shape[0] // 2
    chunk = len(ways) + 1
    while chunk * slots * samples * width > (8 << 20) and chunk % 2 == 0:
        chunk //= 2
    size = chunk * slots * samples * (width + rows) * 2 + pairs * rows * width * 6
    return pl.pallas_call(
        functools.partial(mat_grad_kernel, ways, chunk, len(raw)),
        out_shape=jax.ShapeDtypeStruct((pairs, rows, width), BF16),
        in_specs=[SMEM] * 6 + [VMEM] + [HBM] * (1 + len(raw) + len(links)),
        out_specs=HBM,
        scratch_shapes=[
            pltpu.VMEM((slots, chunk * samples, width), BF16),
            pltpu.VMEM((slots, rows, chunk * samples), BF16),
            pltpu.VMEM((pairs, rows, width), F32),
            pltpu.VMEM((pairs, rows, width), BF16),
            pltpu.SemaphoreType.DMA((chunk, 2 + len(raw))),
            pltpu.SemaphoreType.DMA((pairs // 8,)),
        ],
        compiler_params=limit(56 << 20),
        cost_estimate=CHEAP,
    )(slot_index, slot_width, which, sources, first, owner, grads, own, *raw, *links)


def line_rounds(n):
    order = []
    for i in range(n):
        order.append([(up, k) for k in range(1, n) for up in (True, False) if (i - k >= 0 if up else i + k < n)])
    return order


def shards(embeddings, field_width, pair_fields, pair_mats, labels):
    owners = lax.axis_size("pair")
    groups = lax.axis_size("dp")
    owner = lax.axis_index("pair")
    group = lax.axis_index("dp")
    fields, samples, width = embeddings.shape
    pairs = pair_mats.shape[0]
    every = owners * fields

    pair_list = pair_fields.T
    field_ids = jnp.arange(fields, dtype=jnp.int32)
    slot_ids = jnp.arange(CAP, dtype=jnp.int32)
    picked, near, table = own_rows(owner.reshape(1), pair_list, embeddings, owners)

    mine = lax.dynamic_slice_in_dim(pair_list, owner * pairs, pairs, 1)
    all_ids = jnp.arange(every, dtype=jnp.int32)
    hit = mine.T.reshape(-1)[:, None] == all_ids[None, :]
    wanted = jnp.any(hit, axis=0).astype(jnp.int32).reshape(owners, fields)
    place = jnp.sum(jnp.where(field_ids[:, None] > field_ids[None, :], wanted[:, None, :], 0), axis=2)
    slot_of = jnp.arange(owners, dtype=jnp.int32)[:, None] * CAP + place
    slot_index = jnp.sum(jnp.where(hit, slot_of.reshape(-1)[None, :], 0), axis=1)
    taken = (wanted[:, None, :] > 0) & (place[:, None, :] == slot_ids[None, :, None])
    slot_width = jnp.sum(jnp.where(taken, field_width.reshape(owners, 1, fields), 0), axis=2).reshape(-1)
    own_width = lax.dynamic_slice_in_dim(field_width, owner * fields, fields, 0)

    def chain(own):
        up = lax.ppermute(own, "dp", [(i, i + 1) for i in range(groups - 1)])
        down = lax.ppermute(own, "dp", [(i + 1, i) for i in range(groups - 1)])
        yield [up, down]
        found = [up, down]
        for k in range(2, groups):
            if k == 2:
                found.append(lax.ppermute(up, "dp", [(i, i + 1) for i in range(1, groups - 1)]))
                found.append(lax.ppermute(down, "dp", [(i, i - 1) for i in range(1, groups - 1)]))
            elif 2 * k >= groups:
                ends = [(i, i + k) for i in range(groups - k)]
                found += [lax.ppermute(own, "dp", ends + [(j, i) for i, j in ends])] * 2
            else:
                found.append(lax.ppermute(own, "dp", [(i, i + k) for i in range(groups - k)]))
                found.append(lax.ppermute(own, "dp", [(i + k, i) for i in range(groups - k)]))
        yield found

    def exchange(rows):
        lines = rows.reshape(owners, -1, width)
        return lax.all_to_all(lines, "pair", split_axis=0, concat_axis=0, tiled=True)

    tie = lax.optimization_barrier
    order = line_rounds(groups)
    ways, which, origin = [], [], []
    for r in range(groups - 1):
        names = sorted({order[i][r] for i in range(groups)})
        ways.append([2 * (k - 1) + (not up) for up, k in names])
        which.append([names.index(order[i][r]) for i in range(groups)])
        origin.append([i - order[i][r][1] if order[i][r][0] else i + order[i][r][1] for i in range(groups)])
    places = jnp.array([list(w) + [i] + list(s) for i, (w, s) in enumerate(zip(zip(*which), zip(*origin)))], jnp.int32)
    places = lax.dynamic_index_in_dim(places, group, 0, keepdims=False)
    which, sources = places[: groups - 1], places[groups - 1 :]

    raw_steps = chain(near)
    close = next(raw_steps)
    received = exchange(picked).reshape(owners * CAP, samples, width)
    received, close[:] = tie((received, close))
    raw = next(raw_steps)
    kept_steps = chain(received[:, RAW:])
    sums = forward(slot_index, slot_width, received, pair_mats)
    sums, raw = tie((sums, raw))
    back = exchange(sums)
    near_kept = next(kept_steps)
    raw, near_kept[:] = tie((raw, near_kept))
    far = far_rows(ways, owner.reshape(1), which, table, raw, owners)
    far = [lax.ppermute(x, "pair", [(i, i ^ k) for i in range(owners)]) if k else x for k, x in enumerate(far)]
    kept = next(kept_steps)
    emb_grad, logits, grad = emb_grad_of(table, own_width, back, labels[None, :], fields)
    logits = logits.reshape(samples)
    grads = lax.all_to_all(jnp.broadcast_to(grad, (groups, 1, samples)), "dp", split_axis=0, concat_axis=0, tiled=True)
    rows = width // groups
    mat_grad = mat_grad_of(
        ways, slot_index, slot_width, which, sources, (group * rows).reshape(1), owner.reshape(1), grads, received, far, kept, rows
    )
    return (logits, mat_grad, emb_grad)


def solution(mesh):
    in_specs = (P("pair", "dp", None), P(), P(), P("pair", None, None), P("dp"))
    out_specs = (P("dp"), P("pair", "dp", None), P("pair", "dp", None))
    return jax.shard_map(shards, mesh=mesh, in_specs=in_specs, out_specs=out_specs, check_vma=False)
```

```python
import functools
import math

import jax
import jax.numpy as jnp
from jax import lax
from jax.experimental import pallas as pl
from jax.experimental.pallas import tpu as pltpu
from jax.sharding import PartitionSpec as P

CAP = 3
NOTE = 16
RAW = 64
VMEM = pl.BlockSpec(memory_space=pltpu.VMEM)
SMEM = pl.BlockSpec(memory_space=pltpu.SMEM)
HBM = pl.BlockSpec(memory_space=pl.ANY)
F32 = jnp.float32
BF16 = jnp.bfloat16
CHEAP = pl.CostEstimate(flops=0, bytes_accessed=0, transcendentals=0)


def limit(size):
    return pltpu.CompilerParams(vmem_limit_bytes=size + (4 << 20))


def own_rows_kernel(owner_ref, pairs_ref, rows_ref, out_ref, table_ref, scalar_ref, sems, table_sem):
    fields = rows_ref.shape[0]
    owners = out_ref.shape[0]
    lines, width = out_ref.shape[1] // CAP, out_ref.shape[2]
    total = pairs_ref.shape[1]
    local = pairs_ref[...] - owner_ref[0] * fields
    field = lax.broadcasted_iota(jnp.int32, (fields, total), 0)
    hit = ((local[0:1] == field) | (local[1:2] == field)).astype(BF16)
    low = lax.broadcasted_iota(jnp.int32, (total, 128), 1) * (total // owners)
    at = lax.broadcasted_iota(jnp.int32, (total, 128), 0)
    segment = ((at >= low) & (at < low + total // owners)).astype(BF16)
    needed = jnp.dot(hit, segment, preferred_element_type=F32) > 0
    before = lax.broadcasted_iota(jnp.int32, (fields, fields), 0) > lax.broadcasted_iota(jnp.int32, (fields, fields), 1)
    rank = jnp.dot(before.astype(BF16), needed.astype(BF16), preferred_element_type=F32)
    ids = lax.broadcasted_iota(jnp.int32, (fields, 128), 0).astype(F32)
    rows = lax.broadcasted_iota(jnp.int32, (8, 128), 0)
    table = jnp.zeros((8, 128), F32)
    for c in range(CAP):
        chosen = jnp.sum(jnp.where(needed & (rank == c), ids, 0.0), axis=0, keepdims=True)
        table = jnp.where(rows == c, chosen, table)
    table_ref[...] = table.astype(jnp.int32)
    copy = pltpu.make_async_copy(table_ref, scalar_ref, table_sem)
    copy.start()
    copy.wait()

    def move(d, c, f):
        place = out_ref.at[d, pl.ds(c * lines, lines), :]
        return pltpu.make_async_copy(rows_ref.at[f], place, sems.at[d * CAP + c])

    @pl.loop(0, owners)
    def _(d):
        for c in range(CAP):
            move(d, c, scalar_ref[c, d]).start()

    @pl.loop(0, owners)
    def _(d):
        for c in range(CAP):
            move(d, c, 0).wait()


def own_rows(owner, pair_list, embeddings, owners):
    fields, samples, width = embeddings.shape
    out = (owners, CAP * samples, width)
    return pl.pallas_call(
        own_rows_kernel,
        out_shape=(
            jax.ShapeDtypeStruct(out, BF16),
            jax.ShapeDtypeStruct((8, 128), jnp.int32),
        ),
        in_specs=[SMEM, VMEM, HBM],
        out_specs=(VMEM, VMEM),
        scratch_shapes=[
            pltpu.SMEM((8, 128), jnp.int32),
            pltpu.SemaphoreType.DMA((owners * CAP,)),
            pltpu.SemaphoreType.DMA,
        ],
        compiler_params=limit(56 << 20),
        cost_estimate=CHEAP,
    )(owner, pair_list, embeddings)


def far_rows_kernel(ways, count, owner_ref, which_ref, table_ref, *refs):
    sources, outs, sems = refs[:count], refs[count:-1], refs[-1]
    lines = sources[0].shape[1]

    def move(r, source, k, c, f):
        place = outs[k].at[c, pl.ds(r * lines, lines), :]
        return pltpu.make_async_copy(source.at[f], place, sems.at[r, k * CAP + c])

    for r, choices in enumerate(ways):
        for at, source in enumerate(choices):

            @pl.when((len(choices) == 1) | (which_ref[0] == at))
            def _(r=r, source=source):
                for k in range(len(outs)):
                    for c in range(CAP):
                        move(r, sources[source], k, c, table_ref[c, owner_ref[0] ^ k]).start()

    for r in range(len(ways)):
        for k in range(len(outs)):
            for c in range(CAP):
                move(r, sources[0], k, c, 0).wait()


def far_rows(ways, owner, which, table, sources, owners):
    _, lines, width = sources[0].shape
    shape = (CAP, len(ways) * lines, width)
    return pl.pallas_call(
        functools.partial(far_rows_kernel, ways, len(sources)),
        out_shape=[jax.ShapeDtypeStruct(shape, BF16)] * owners,
        in_specs=[SMEM, SMEM, SMEM] + [HBM] * len(sources),
        out_specs=[VMEM] * owners,
        scratch_shapes=[pltpu.SemaphoreType.DMA((len(ways), owners * CAP))],
        compiler_params=limit(56 << 20),
        cost_estimate=CHEAP,
    )(owner, which, table, *sources)


def forward_kernel(group, slot_ref, width_ref, rows_ref, mats_ref, sums_ref, x_ref, u_ref, acc_ref, mats, sems):
    slots, samples, width = x_ref.shape
    steps = mats.shape[0] // group

    def load(i):
        part = pl.ds(i * group, group)
        return pltpu.make_async_copy(mats_ref.at[part], mats.at[part], sems.at[i])

    for i in range(steps):
        load(i).start()
    columns = lax.broadcasted_iota(jnp.int32, (samples, width), 1)

    @pl.loop(0, slots, unroll=4)
    def _(j):
        x_ref[j] = jnp.where(columns < width_ref[j], rows_ref[j], jnp.zeros_like(rows_ref[j]))
        u_ref[j] = jnp.zeros((samples, width), F32)

    acc_ref[...] = jnp.zeros_like(acc_ref)

    @pl.loop(0, steps)
    def _(i):
        load(i).wait()
        acc = jnp.zeros((samples, width), F32)
        for k in range(group):
            p = i * group + k
            a, b = slot_ref[2 * p], slot_ref[2 * p + 1]
            left, right, mat = x_ref[a], x_ref[b], mats[p]
            projected = jnp.dot(left, mat, preferred_element_type=F32)
            back = lax.dot_general(right, mat, (((1,), (1,)), ((), ())), preferred_element_type=F32)
            acc += projected * right.astype(F32)
            u_ref[b] += projected
            u_ref[a] += back
        acc_ref[...] += acc

    total = acc_ref[:, 0:128]
    for at in range(128, width, 128):
        total = total + acc_ref[:, at : at + 128]
    part = jnp.sum(total.T, axis=0, keepdims=True)
    note = jnp.zeros((NOTE, width), F32)
    for row in range(3):
        piece = part.astype(BF16).astype(F32)
        part = part - piece
        at = lax.broadcasted_iota(jnp.int32, (NOTE, width), 0) == row
        note = jnp.where(at, jnp.concatenate([piece] * (width // samples), axis=1), note)
    lines = CAP * samples

    @pl.loop(0, slots // CAP)
    def _(o):
        for c in range(CAP):
            sums_ref[o, c * samples : (c + 1) * samples, :] = u_ref[o * CAP + c].astype(BF16)
        sums_ref[o, lines : lines + NOTE, :] = note.astype(BF16)


def forward(slot_index, slot_width, rows, mats, group=8):
    slots, samples, width = rows.shape
    sums = (slots // CAP, CAP * samples + NOTE, width)
    return pl.pallas_call(
        functools.partial(forward_kernel, group),
        out_shape=jax.ShapeDtypeStruct(sums, BF16),
        in_specs=[SMEM, SMEM, VMEM, HBM],
        out_specs=VMEM,
        scratch_shapes=[
            pltpu.VMEM(rows.shape, BF16),
            pltpu.VMEM(rows.shape, F32),
            pltpu.VMEM((samples, width), F32),
            pltpu.VMEM(mats.shape, BF16),
            pltpu.SemaphoreType.DMA((mats.shape[0] // group,)),
        ],
        compiler_params=limit(52 << 20),
        cost_estimate=CHEAP,
    )(slot_index, slot_width, rows, mats)


def factor_kernel(back_ref, labels_ref, logit_ref, grad_ref):
    samples = logit_ref.shape[1]
    lines = back_ref.shape[1] - NOTE
    note = jnp.sum(back_ref[:, lines : lines + NOTE, 0:samples].astype(F32), axis=0)
    logit = note[0:1] + note[1:2] + note[2:3]
    logit_ref[...] = logit
    grad = jax.nn.sigmoid(logit) - labels_ref[...].astype(F32)
    for g in range(grad_ref.shape[0]):
        grad_ref[g] = grad


def factor_of(back, labels, groups):
    samples = labels.shape[1]
    return pl.pallas_call(
        factor_kernel,
        out_shape=(jax.ShapeDtypeStruct((1, samples), F32), jax.ShapeDtypeStruct((groups, 1, samples), F32)),
        in_specs=[VMEM, VMEM],
        out_specs=(VMEM, VMEM),
        compiler_params=limit(math.prod(back.shape) * 2),
        cost_estimate=CHEAP,
    )(back, labels)


def emb_grad_kernel(table_ref, width_ref, back_ref, grad_ref, out_ref):
    fields, samples, width = out_ref.shape
    owners = back_ref.shape[0]

    @pl.loop(0, fields)
    def _(f):
        out_ref[f] = jnp.zeros((samples, width), F32)

    @pl.loop(0, owners)
    def _(o):
        for c in range(CAP):
            f = table_ref[c, o]
            out_ref[f] += back_ref[o, c * samples : (c + 1) * samples, :].astype(F32)

    factor = jnp.broadcast_to(grad_ref[0], (128, samples)).T
    factor = jnp.concatenate([factor] * (width // 128), axis=1)
    columns = lax.broadcasted_iota(jnp.int32, (samples, width), 1)

    @pl.loop(0, fields)
    def _(f):
        out_ref[f] = jnp.where(columns < width_ref[f], out_ref[f] * factor, 0.0)


def emb_grad_of(table, own_width, back, grad, fields):
    samples, width = grad.shape[2], back.shape[2]
    return pl.pallas_call(
        emb_grad_kernel,
        out_shape=jax.ShapeDtypeStruct((fields, samples, width), F32),
        in_specs=[SMEM, SMEM, VMEM, VMEM],
        out_specs=VMEM,
        compiler_params=limit(math.prod(back.shape) * 2 + fields * samples * width * 4),
        cost_estimate=CHEAP,
    )(table, own_width, back, grad)


def mat_grad_kernel(ways, chunk, owners, slot_ref, width_ref, which_ref, source_ref, first_ref, owner_ref, grads_ref, own_ref, *refs):
    raws = refs[:owners]
    *links, out_ref, x_ref, t_ref, acc_ref, done_ref, sems, done_sems = refs[owners:]
    group = done_ref.shape[0] // done_sems.shape[0]
    count = len(ways) + 1
    width = x_ref.shape[2]
    slots, samples, _ = own_ref.shape
    kept_lines = links[0].shape[1]
    raw_lines = samples - kept_lines
    pairs, rows, _ = acc_ref.shape
    own_row = lax.broadcasted_iota(jnp.int32, (rows, width), 0) + first_ref[0]
    columns = lax.broadcasted_iota(jnp.int32, (rows, width), 1)
    pick = (columns == own_row).astype(BF16)

    def place(k, low, size):
        return x_ref.at[:, pl.ds(k * samples + low, size), :]

    def store(i):
        part = pl.ds(i * group, group)
        return pltpu.make_async_copy(done_ref.at[part], out_ref.at[part], done_sems.at[i])

    for start in range(0, count, chunk):
        waits = [[] for _ in range(chunk)]
        for k in range(chunk):
            if start + k == 0:
                waits[k].append(pltpu.make_async_copy(own_ref, place(k, 0, samples), sems.at[k, 0]))
                waits[k][-1].start()
                continue
            r = start + k - 1
            for d in range(owners):
                raw = raws[d].at[:, pl.ds(r * raw_lines, raw_lines), :]
                spot = x_ref.at[pl.ds((owner_ref[0] ^ d) * CAP, CAP), pl.ds(k * samples, raw_lines), :]
                waits[k].append(pltpu.make_async_copy(raw, spot, sems.at[k, 2 + d]))
                waits[k][-1].start()
            for at, link in enumerate(ways[r]):

                @pl.when((len(ways[r]) == 1) | (which_ref[0] == at))
                def _(k=k, link=link):
                    pltpu.make_async_copy(links[link], place(k, raw_lines, kept_lines), sems.at[k, 1]).start()

            waits[k].append(pltpu.make_async_copy(links[0], place(k, raw_lines, kept_lines), sems.at[k, 1]))
        for k in range(chunk):
            for copy in waits[k]:
                copy.wait()
            grad = grads_ref[source_ref[start + k]]

            @pl.loop(0, slots, unroll=12)
            def _(j, k=k, grad=grad):
                x = x_ref[j, k * samples : (k + 1) * samples, :]
                turned = lax.dot_general(pick, x, (((1,), (1,)), ((), ())), preferred_element_type=F32)
                t_ref[j, :, k * samples : (k + 1) * samples] = (turned * grad).astype(BF16)

        def term_of(p):
            a, b = slot_ref[2 * p], slot_ref[2 * p + 1]
            term = jnp.dot(t_ref[a], x_ref[b], preferred_element_type=F32)
            return term if start == 0 else term + acc_ref[p]

        if start + chunk < count:

            @pl.loop(0, pairs, unroll=8)
            def _(p, term_of=term_of):
                acc_ref[p] = term_of(p)

            continue

        @pl.loop(0, pairs // group)
        def _(i, term_of=term_of):
            for k in range(group):
                p = i * group + k
                a, b = slot_ref[2 * p], slot_ref[2 * p + 1]
                kept = (own_row < width_ref[a]) & (columns < width_ref[b])
                done_ref[p] = jnp.where(kept, term_of(p), 0.0).astype(BF16)
            store(i).start()

        @pl.loop(0, pairs // group)
        def _(i):
            store(i).wait()


def mat_grad_of(ways, slot_index, slot_width, which, sources, first, owner, grads, own, raw, links, rows):
    slots, samples, width = own.shape
    pairs = slot_index.shape[0] // 2
    chunk = len(ways) + 1
    while chunk * slots * samples * width > (8 << 20) and chunk % 2 == 0:
        chunk //= 2
    size = chunk * slots * samples * (width + rows) * 2 + pairs * rows * width * 6
    return pl.pallas_call(
        functools.partial(mat_grad_kernel, ways, chunk, len(raw)),
        out_shape=jax.ShapeDtypeStruct((pairs, rows, width), BF16),
        in_specs=[SMEM] * 6 + [VMEM] + [HBM] * (1 + len(raw) + len(links)),
        out_specs=HBM,
        scratch_shapes=[
            pltpu.VMEM((slots, chunk * samples, width), BF16),
            pltpu.VMEM((slots, rows, chunk * samples), BF16),
            pltpu.VMEM((pairs, rows, width), F32),
            pltpu.VMEM((pairs, rows, width), BF16),
            pltpu.SemaphoreType.DMA((chunk, 2 + len(raw))),
            pltpu.SemaphoreType.DMA((pairs // 8,)),
        ],
        compiler_params=limit(56 << 20),
        cost_estimate=CHEAP,
    )(slot_index, slot_width, which, sources, first, owner, grads, own, *raw, *links)


def shards(embeddings, field_width, pair_fields, pair_mats, labels):
    owners = lax.axis_size("pair")
    groups = lax.axis_size("dp")
    owner = lax.axis_index("pair")
    group = lax.axis_index("dp")
    fields, samples, width = embeddings.shape
    pairs = pair_mats.shape[0]
    every = owners * fields

    pair_list = pair_fields.T
    field_ids = jnp.arange(fields, dtype=jnp.int32)
    slot_ids = jnp.arange(CAP, dtype=jnp.int32)
    picked, table = own_rows(owner.reshape(1), pair_list, embeddings, owners)

    mine = lax.dynamic_slice_in_dim(pair_list, owner * pairs, pairs, 1)
    all_ids = jnp.arange(every, dtype=jnp.int32)
    hit = mine.T.reshape(-1)[:, None] == all_ids[None, :]
    wanted = jnp.any(hit, axis=0).astype(jnp.int32).reshape(owners, fields)
    place = jnp.sum(jnp.where(field_ids[:, None] > field_ids[None, :], wanted[:, None, :], 0), axis=2)
    slot_of = jnp.arange(owners, dtype=jnp.int32)[:, None] * CAP + place
    slot_index = jnp.sum(jnp.where(hit, slot_of.reshape(-1)[None, :], 0), axis=1)
    taken = (wanted[:, None, :] > 0) & (place[:, None, :] == slot_ids[None, :, None])
    slot_width = jnp.sum(jnp.where(taken, field_width.reshape(owners, 1, fields), 0), axis=2).reshape(-1)
    own_width = lax.dynamic_slice_in_dim(field_width, owner * fields, fields, 0)

    def swap(rows, k, members=range(groups)):
        return lax.ppermute(rows, "dp", [(i, i ^ k) for i in members])

    def chain(own):
        if groups != 4:
            found = [swap(own, k) for k in range(1, groups)]
            yield found
            yield found
            return
        beside, across = swap(own, 1), swap(own, 3)
        yield [beside, across]
        yield [beside, across, swap(beside, 3, (1, 2)), swap(across, 1, (1, 2))]

    def exchange(rows):
        lines = rows.reshape(owners, -1, width)
        return lax.all_to_all(lines, "pair", split_axis=0, concat_axis=0, tiled=True)

    tie = lax.optimization_barrier
    ways = [[0], [1], [2, 3]] if groups == 4 else [[k] for k in range(groups - 1)]
    steps = (1, 3, 2) if groups == 4 else range(1, groups)
    which = ((group == 0) | (group == 3)).astype(jnp.int32).reshape(1)
    sources = jnp.stack([group] + [group ^ k for k in steps]).astype(jnp.int32)

    raw_steps = chain(embeddings[:, :RAW])
    close = next(raw_steps)
    received = exchange(picked).reshape(owners * CAP, samples, width)
    received, close[:] = tie((received, close))
    raw = next(raw_steps)
    kept_steps = chain(received[:, RAW:])
    sums = forward(slot_index, slot_width, received, pair_mats)
    sums, raw = tie((sums, raw))
    back = exchange(sums)
    near_kept = next(kept_steps)
    far = far_rows(ways, owner.reshape(1), which, table, raw, owners)
    first = [k for k in range(2, owners, 2)]
    moved = {k: lax.ppermute(far[k], "pair", [(i, i ^ k) for i in range(owners)]) for k in first}
    rest = [k for k in range(owners - 1, 0, -1) if k not in first]
    if owners == 8:
        moved, far = tie((moved, far))
    moved |= {k: lax.ppermute(far[k], "pair", [(i, i ^ k) for i in range(owners)]) for k in rest}
    far = [moved.get(k, far[k]) for k in range(owners)]
    kept = next(kept_steps)
    back, near_kept[:] = tie((back, near_kept))
    logits, grad = factor_of(back, labels[None, :], groups)
    logits = logits.reshape(samples)
    grads = lax.all_to_all(grad, "dp", split_axis=0, concat_axis=0, tiled=True)
    emb_grad = emb_grad_of(table, own_width, back, grad, fields)
    rows = width // groups
    mat_grad = mat_grad_of(
        ways, slot_index, slot_width, which, sources, (group * rows).reshape(1), owner.reshape(1), grads, received, far, kept, rows
    )
    return (logits, mat_grad, emb_grad)


def solution(mesh):
    in_specs = (P("pair", "dp", None), P(), P(), P("pair", None, None), P("dp"))
    out_specs = (P("dp"), P("pair", "dp", None), P("pair", "dp", None))
    return jax.shard_map(shards, mesh=mesh, in_specs=in_specs, out_specs=out_specs, check_vma=False)
```

```python
import functools
import math

import jax
import jax.numpy as jnp
from jax import lax
from jax.experimental import pallas as pl
from jax.experimental.pallas import tpu as pltpu
from jax.sharding import PartitionSpec as P

CAP = 3
NOTE = 16
RAW = 64
VMEM = pl.BlockSpec(memory_space=pltpu.VMEM)
SMEM = pl.BlockSpec(memory_space=pltpu.SMEM)
HBM = pl.BlockSpec(memory_space=pl.ANY)
F32 = jnp.float32
BF16 = jnp.bfloat16
CHEAP = pl.CostEstimate(flops=0, bytes_accessed=0, transcendentals=0)


def limit(size):
    return pltpu.CompilerParams(vmem_limit_bytes=size + (4 << 20))


def own_rows_kernel(owner_ref, pairs_ref, rows_ref, out_ref, table_ref, held_ref, scalar_ref, sems, table_sem, load_sem):
    fields = rows_ref.shape[0]
    owners = out_ref.shape[0]
    lines, width = out_ref.shape[1] // CAP, out_ref.shape[2]
    total = pairs_ref.shape[1]
    load = pltpu.make_async_copy(rows_ref, held_ref, load_sem)
    load.start()
    local = pairs_ref[...] - owner_ref[0] * fields
    field = lax.broadcasted_iota(jnp.int32, (fields, total), 0)
    hit = ((local[0:1] == field) | (local[1:2] == field)).astype(BF16)
    low = lax.broadcasted_iota(jnp.int32, (total, 128), 1) * (total // owners)
    at = lax.broadcasted_iota(jnp.int32, (total, 128), 0)
    segment = ((at >= low) & (at < low + total // owners)).astype(BF16)
    needed = jnp.dot(hit, segment, preferred_element_type=F32) > 0
    before = lax.broadcasted_iota(jnp.int32, (fields, fields), 0) > lax.broadcasted_iota(jnp.int32, (fields, fields), 1)
    rank = jnp.dot(before.astype(BF16), needed.astype(BF16), preferred_element_type=F32)
    ids = lax.broadcasted_iota(jnp.int32, (fields, 128), 0).astype(F32)
    rows = lax.broadcasted_iota(jnp.int32, (8, 128), 0)
    table = jnp.zeros((8, 128), F32)
    for c in range(CAP):
        chosen = jnp.sum(jnp.where(needed & (rank == c), ids, 0.0), axis=0, keepdims=True)
        table = jnp.where(rows == c, chosen, table)
    table_ref[...] = table.astype(jnp.int32)
    copy = pltpu.make_async_copy(table_ref, scalar_ref, table_sem)
    copy.start()
    copy.wait()
    load.wait()

    def move(d, c, f):
        place = out_ref.at[d, pl.ds(c * lines, lines), :]
        return pltpu.make_async_copy(held_ref.at[f], place, sems.at[d * CAP + c])

    @pl.loop(0, owners)
    def _(d):
        for c in range(CAP):
            move(d, c, scalar_ref[c, d]).start()

    @pl.loop(0, owners)
    def _(d):
        for c in range(CAP):
            move(d, c, 0).wait()


def own_rows(owner, pair_list, embeddings, owners):
    fields, samples, width = embeddings.shape
    out = (owners, CAP * samples, width)
    return pl.pallas_call(
        own_rows_kernel,
        out_shape=(
            jax.ShapeDtypeStruct(out, BF16),
            jax.ShapeDtypeStruct((8, 128), jnp.int32),
        ),
        in_specs=[SMEM, VMEM, HBM],
        out_specs=(HBM, VMEM),
        scratch_shapes=[
            pltpu.VMEM(embeddings.shape, BF16),
            pltpu.SMEM((8, 128), jnp.int32),
            pltpu.SemaphoreType.DMA((owners * CAP,)),
            pltpu.SemaphoreType.DMA,
            pltpu.SemaphoreType.DMA,
        ],
        compiler_params=limit(56 << 20),
        cost_estimate=CHEAP,
    )(owner, pair_list, embeddings)


def far_rows_kernel(ways, count, owner_ref, which_ref, table_ref, *refs):
    sources, outs, (held_ref, sems, load_sems) = refs[:count], refs[count:-3], refs[-3:]
    lines = sources[0].shape[1]

    def move(r, k, c, f):
        place = outs[k].at[c, pl.ds(r * lines, lines), :]
        return pltpu.make_async_copy(held_ref.at[r, f], place, sems.at[r, k * CAP + c])

    def load(r, source):
        return pltpu.make_async_copy(source, held_ref.at[r], load_sems.at[r])

    for r, choices in enumerate(ways):
        for at, source in enumerate(choices):

            @pl.when((len(choices) == 1) | (which_ref[0] == at))
            def _(r=r, source=source):
                load(r, sources[source]).start()

    for r in range(len(ways)):
        load(r, sources[0]).wait()
        for k in range(len(outs)):
            for c in range(CAP):
                move(r, k, c, table_ref[c, owner_ref[0] ^ k]).start()

    for r in range(len(ways)):
        for k in range(len(outs)):
            for c in range(CAP):
                move(r, k, c, 0).wait()


def far_rows(ways, owner, which, table, sources, owners):
    _, lines, width = sources[0].shape
    shape = (CAP, len(ways) * lines, width)
    return pl.pallas_call(
        functools.partial(far_rows_kernel, ways, len(sources)),
        out_shape=[jax.ShapeDtypeStruct(shape, BF16)] * owners,
        in_specs=[SMEM, SMEM, SMEM] + [HBM] * len(sources),
        out_specs=[HBM] * owners,
        scratch_shapes=[
            pltpu.VMEM((len(ways), *sources[0].shape), BF16),
            pltpu.SemaphoreType.DMA((len(ways), owners * CAP)),
            pltpu.SemaphoreType.DMA((len(ways),)),
        ],
        compiler_params=limit(56 << 20),
        cost_estimate=CHEAP,
    )(owner, which, table, *sources)


def forward_kernel(group, slot_ref, width_ref, rows_ref, mats_ref, sums_ref, x_ref, u_ref, acc_ref, mats, sems):
    slots, samples, width = x_ref.shape
    steps = mats.shape[0] // group

    def load(i):
        part = pl.ds(i * group, group)
        return pltpu.make_async_copy(mats_ref.at[part], mats.at[part], sems.at[i])

    for i in range(steps):
        load(i).start()
    columns = lax.broadcasted_iota(jnp.int32, (samples, width), 1)

    @pl.loop(0, slots, unroll=4)
    def _(j):
        x_ref[j] = jnp.where(columns < width_ref[j], rows_ref[j], jnp.zeros_like(rows_ref[j]))
        u_ref[j] = jnp.zeros((samples, width), F32)

    acc_ref[...] = jnp.zeros_like(acc_ref)

    @pl.loop(0, steps)
    def _(i):
        load(i).wait()
        acc = jnp.zeros((samples, width), F32)
        for k in range(group):
            p = i * group + k
            a, b = slot_ref[2 * p], slot_ref[2 * p + 1]
            left, right, mat = x_ref[a], x_ref[b], mats[p]
            projected = jnp.dot(left, mat, preferred_element_type=F32)
            back = lax.dot_general(right, mat, (((1,), (1,)), ((), ())), preferred_element_type=F32)
            acc += projected * right.astype(F32)
            u_ref[b] += projected
            u_ref[a] += back
        acc_ref[...] += acc

    total = acc_ref[:, 0:128]
    for at in range(128, width, 128):
        total = total + acc_ref[:, at : at + 128]
    part = jnp.sum(total.T, axis=0, keepdims=True)
    note = jnp.zeros((NOTE, width), F32)
    for row in range(3):
        piece = part.astype(BF16).astype(F32)
        part = part - piece
        at = lax.broadcasted_iota(jnp.int32, (NOTE, width), 0) == row
        note = jnp.where(at, jnp.concatenate([piece] * (width // samples), axis=1), note)
    lines = CAP * samples

    @pl.loop(0, slots // CAP)
    def _(o):
        for c in range(CAP):
            sums_ref[o, c * samples : (c + 1) * samples, :] = u_ref[o * CAP + c].astype(BF16)
        sums_ref[o, lines : lines + NOTE, :] = note.astype(BF16)


def forward(slot_index, slot_width, rows, mats, group=8):
    slots, samples, width = rows.shape
    sums = (slots // CAP, CAP * samples + NOTE, width)
    return pl.pallas_call(
        functools.partial(forward_kernel, group),
        out_shape=jax.ShapeDtypeStruct(sums, BF16),
        in_specs=[SMEM, SMEM, VMEM, HBM],
        out_specs=VMEM,
        scratch_shapes=[
            pltpu.VMEM(rows.shape, BF16),
            pltpu.VMEM(rows.shape, F32),
            pltpu.VMEM((samples, width), F32),
            pltpu.VMEM(mats.shape, BF16),
            pltpu.SemaphoreType.DMA((mats.shape[0] // group,)),
        ],
        compiler_params=limit(52 << 20),
        cost_estimate=CHEAP,
    )(slot_index, slot_width, rows, mats)


def factor_kernel(back_ref, labels_ref, logit_ref, grad_ref):
    samples = logit_ref.shape[1]
    lines = back_ref.shape[1] - NOTE
    note = jnp.sum(back_ref[:, lines : lines + NOTE, 0:samples].astype(F32), axis=0)
    logit = note[0:1] + note[1:2] + note[2:3]
    logit_ref[...] = logit
    grad = jax.nn.sigmoid(logit) - labels_ref[...].astype(F32)
    for g in range(grad_ref.shape[0]):
        grad_ref[g] = grad


def factor_of(back, labels, groups):
    samples = labels.shape[1]
    return pl.pallas_call(
        factor_kernel,
        out_shape=(jax.ShapeDtypeStruct((1, samples), F32), jax.ShapeDtypeStruct((groups, 1, samples), F32)),
        in_specs=[VMEM, VMEM],
        out_specs=(VMEM, VMEM),
        compiler_params=limit(math.prod(back.shape) * 2),
        cost_estimate=CHEAP,
    )(back, labels)


def emb_grad_kernel(table_ref, width_ref, back_ref, grad_ref, out_ref):
    fields, samples, width = out_ref.shape
    owners = back_ref.shape[0]

    @pl.loop(0, fields)
    def _(f):
        out_ref[f] = jnp.zeros((samples, width), F32)

    @pl.loop(0, owners)
    def _(o):
        for c in range(CAP):
            f = table_ref[c, o]
            out_ref[f] += back_ref[o, c * samples : (c + 1) * samples, :].astype(F32)

    factor = jnp.broadcast_to(grad_ref[0], (128, samples)).T
    factor = jnp.concatenate([factor] * (width // 128), axis=1)
    columns = lax.broadcasted_iota(jnp.int32, (samples, width), 1)

    @pl.loop(0, fields)
    def _(f):
        out_ref[f] = jnp.where(columns < width_ref[f], out_ref[f] * factor, 0.0)


def emb_grad_of(table, own_width, back, grad, fields):
    samples, width = grad.shape[2], back.shape[2]
    return pl.pallas_call(
        emb_grad_kernel,
        out_shape=jax.ShapeDtypeStruct((fields, samples, width), F32),
        in_specs=[SMEM, SMEM, VMEM, VMEM],
        out_specs=VMEM,
        compiler_params=limit(math.prod(back.shape) * 2 + fields * samples * width * 4),
        cost_estimate=CHEAP,
    )(table, own_width, back, grad)


def mat_grad_kernel(ways, chunk, owners, slot_ref, width_ref, which_ref, source_ref, first_ref, owner_ref, grads_ref, own_ref, *refs):
    raws = refs[:owners]
    *links, out_ref, x_ref, t_ref, acc_ref, done_ref, sems, done_sems = refs[owners:]
    group = done_ref.shape[0] // done_sems.shape[0]
    count = len(ways) + 1
    width = x_ref.shape[2]
    slots, samples, _ = own_ref.shape
    kept_lines = links[0].shape[1]
    raw_lines = samples - kept_lines
    pairs, rows, _ = acc_ref.shape
    own_row = lax.broadcasted_iota(jnp.int32, (rows, width), 0) + first_ref[0]
    columns = lax.broadcasted_iota(jnp.int32, (rows, width), 1)
    pick = (columns == own_row).astype(BF16)

    def place(k, low, size):
        return x_ref.at[:, pl.ds(k * samples + low, size), :]

    def store(i):
        part = pl.ds(i * group, group)
        return pltpu.make_async_copy(done_ref.at[part], out_ref.at[part], done_sems.at[i])

    for start in range(0, count, chunk):
        waits = [[] for _ in range(chunk)]
        for k in range(chunk):
            if start + k == 0:
                waits[k].append(pltpu.make_async_copy(own_ref, place(k, 0, samples), sems.at[k, 0]))
                waits[k][-1].start()
                continue
            r = start + k - 1
            for d in range(owners):
                raw = raws[d].at[:, pl.ds(r * raw_lines, raw_lines), :]
                spot = x_ref.at[pl.ds((owner_ref[0] ^ d) * CAP, CAP), pl.ds(k * samples, raw_lines), :]
                waits[k].append(pltpu.make_async_copy(raw, spot, sems.at[k, 2 + d]))
                waits[k][-1].start()
            for at, link in enumerate(ways[r]):

                @pl.when((len(ways[r]) == 1) | (which_ref[0] == at))
                def _(k=k, link=link):
                    pltpu.make_async_copy(links[link], place(k, raw_lines, kept_lines), sems.at[k, 1]).start()

            waits[k].append(pltpu.make_async_copy(links[0], place(k, raw_lines, kept_lines), sems.at[k, 1]))
        for k in range(chunk):
            for copy in waits[k]:
                copy.wait()
            grad = grads_ref[source_ref[start + k]]

            @pl.loop(0, slots, unroll=12)
            def _(j, k=k, grad=grad):
                x = x_ref[j, k * samples : (k + 1) * samples, :]
                turned = lax.dot_general(pick, x, (((1,), (1,)), ((), ())), preferred_element_type=F32)
                t_ref[j, :, k * samples : (k + 1) * samples] = (turned * grad).astype(BF16)

        def term_of(p):
            a, b = slot_ref[2 * p], slot_ref[2 * p + 1]
            term = jnp.dot(t_ref[a], x_ref[b], preferred_element_type=F32)
            return term if start == 0 else term + acc_ref[p]

        if start + chunk < count:

            @pl.loop(0, pairs, unroll=8)
            def _(p, term_of=term_of):
                acc_ref[p] = term_of(p)

            continue

        @pl.loop(0, pairs // group)
        def _(i, term_of=term_of):
            for k in range(group):
                p = i * group + k
                a, b = slot_ref[2 * p], slot_ref[2 * p + 1]
                kept = (own_row < width_ref[a]) & (columns < width_ref[b])
                done_ref[p] = jnp.where(kept, term_of(p), 0.0).astype(BF16)
            store(i).start()

        @pl.loop(0, pairs // group)
        def _(i):
            store(i).wait()


def mat_grad_of(ways, slot_index, slot_width, which, sources, first, owner, grads, own, raw, links, rows):
    slots, samples, width = own.shape
    pairs = slot_index.shape[0] // 2
    chunk = len(ways) + 1
    while chunk * slots * samples * width > (8 << 20) and chunk % 2 == 0:
        chunk //= 2
    size = chunk * slots * samples * (width + rows) * 2 + pairs * rows * width * 6
    return pl.pallas_call(
        functools.partial(mat_grad_kernel, ways, chunk, len(raw)),
        out_shape=jax.ShapeDtypeStruct((pairs, rows, width), BF16),
        in_specs=[SMEM] * 6 + [VMEM] + [HBM] * (1 + len(raw) + len(links)),
        out_specs=HBM,
        scratch_shapes=[
            pltpu.VMEM((slots, chunk * samples, width), BF16),
            pltpu.VMEM((slots, rows, chunk * samples), BF16),
            pltpu.VMEM((pairs, rows, width), F32),
            pltpu.VMEM((pairs, rows, width), BF16),
            pltpu.SemaphoreType.DMA((chunk, 2 + len(raw))),
            pltpu.SemaphoreType.DMA((pairs // 8,)),
        ],
        compiler_params=limit(56 << 20),
        cost_estimate=CHEAP,
    )(slot_index, slot_width, which, sources, first, owner, grads, own, *raw, *links)


def shards(embeddings, field_width, pair_fields, pair_mats, labels):
    owners = lax.axis_size("pair")
    groups = lax.axis_size("dp")
    owner = lax.axis_index("pair")
    group = lax.axis_index("dp")
    fields, samples, width = embeddings.shape
    pairs = pair_mats.shape[0]
    every = owners * fields

    pair_list = pair_fields.T
    field_ids = jnp.arange(fields, dtype=jnp.int32)
    slot_ids = jnp.arange(CAP, dtype=jnp.int32)
    picked, table = own_rows(owner.reshape(1), pair_list, embeddings, owners)

    mine = lax.dynamic_slice_in_dim(pair_list, owner * pairs, pairs, 1)
    all_ids = jnp.arange(every, dtype=jnp.int32)
    hit = mine.T.reshape(-1)[:, None] == all_ids[None, :]
    wanted = jnp.any(hit, axis=0).astype(jnp.int32).reshape(owners, fields)
    place = jnp.sum(jnp.where(field_ids[:, None] > field_ids[None, :], wanted[:, None, :], 0), axis=2)
    slot_of = jnp.arange(owners, dtype=jnp.int32)[:, None] * CAP + place
    slot_index = jnp.sum(jnp.where(hit, slot_of.reshape(-1)[None, :], 0), axis=1)
    taken = (wanted[:, None, :] > 0) & (place[:, None, :] == slot_ids[None, :, None])
    slot_width = jnp.sum(jnp.where(taken, field_width.reshape(owners, 1, fields), 0), axis=2).reshape(-1)
    own_width = lax.dynamic_slice_in_dim(field_width, owner * fields, fields, 0)

    def swap(rows, k, members=range(groups)):
        return lax.ppermute(rows, "dp", [(i, i ^ k) for i in members])

    def chain(own):
        if groups != 4:
            found = [swap(own, k) for k in range(1, groups)]
            yield found
            yield found
            return
        beside, across = swap(own, 1), swap(own, 3)
        yield [beside, across]
        yield [beside, across, swap(beside, 3, (1, 2)), swap(across, 1, (1, 2))]

    def exchange(rows):
        lines = rows.reshape(owners, -1, width)
        return lax.all_to_all(lines, "pair", split_axis=0, concat_axis=0, tiled=True)

    tie = lax.optimization_barrier
    ways = [[0], [1], [2, 3]] if groups == 4 else [[k] for k in range(groups - 1)]
    steps = (1, 3, 2) if groups == 4 else range(1, groups)
    which = ((group == 0) | (group == 3)).astype(jnp.int32).reshape(1)
    sources = jnp.stack([group] + [group ^ k for k in steps]).astype(jnp.int32)

    raw_steps = chain(embeddings[:, :RAW])
    close = next(raw_steps)
    received = exchange(picked).reshape(owners * CAP, samples, width)
    received, close[:] = tie((received, close))
    raw = next(raw_steps)
    kept_steps = chain(received[:, RAW:])
    sums = forward(slot_index, slot_width, received, pair_mats)
    sums, raw = tie((sums, raw))
    back = exchange(sums)
    near_kept = next(kept_steps)
    far = far_rows(ways, owner.reshape(1), which, table, raw, owners)
    first = [k for k in range(2, owners, 2)]
    moved = {k: lax.ppermute(far[k], "pair", [(i, i ^ k) for i in range(owners)]) for k in first}
    rest = [k for k in range(owners - 1, 0, -1) if k not in first]
    if owners == 8:
        moved, far = tie((moved, far))
    moved |= {k: lax.ppermute(far[k], "pair", [(i, i ^ k) for i in range(owners)]) for k in rest}
    far = [moved.get(k, far[k]) for k in range(owners)]
    kept = next(kept_steps)
    back, near_kept[:] = tie((back, near_kept))
    logits, grad = factor_of(back, labels[None, :], groups)
    logits = logits.reshape(samples)
    grads = lax.all_to_all(grad, "dp", split_axis=0, concat_axis=0, tiled=True)
    emb_grad = emb_grad_of(table, own_width, back, grad, fields)
    rows = width // groups
    mat_grad = mat_grad_of(
        ways, slot_index, slot_width, which, sources, (group * rows).reshape(1), owner.reshape(1), grads, received, far, kept, rows
    )
    return (logits, mat_grad, emb_grad)


def solution(mesh):
    in_specs = (P("pair", "dp", None), P(), P(), P("pair", None, None), P("dp"))
    out_specs = (P("dp"), P("pair", "dp", None), P("pair", "dp", None))
    return jax.shard_map(shards, mesh=mesh, in_specs=in_specs, out_specs=out_specs, check_vma=False)
```

```python
import functools
import math

import jax
import jax.numpy as jnp
from jax import lax
from jax.experimental import pallas as pl
from jax.experimental.pallas import tpu as pltpu
from jax.sharding import PartitionSpec as P

CAP = 3
NOTE = 16
RAW = 64
VMEM = pl.BlockSpec(memory_space=pltpu.VMEM)
SMEM = pl.BlockSpec(memory_space=pltpu.SMEM)
HBM = pl.BlockSpec(memory_space=pl.ANY)
F32 = jnp.float32
BF16 = jnp.bfloat16
CHEAP = pl.CostEstimate(flops=0, bytes_accessed=0, transcendentals=0)


def limit(size):
    return pltpu.CompilerParams(vmem_limit_bytes=size + (4 << 20))


def own_rows_kernel(owner_ref, pairs_ref, rows_ref, out_ref, table_ref, held_ref, scalar_ref, sems, table_sem, load_sem):
    fields = rows_ref.shape[0]
    owners = out_ref.shape[0]
    lines, width = out_ref.shape[1] // CAP, out_ref.shape[2]
    total = pairs_ref.shape[1]
    load = pltpu.make_async_copy(rows_ref, held_ref, load_sem)
    load.start()
    local = pairs_ref[...] - owner_ref[0] * fields
    field = lax.broadcasted_iota(jnp.int32, (fields, total), 0)
    hit = ((local[0:1] == field) | (local[1:2] == field)).astype(BF16)
    low = lax.broadcasted_iota(jnp.int32, (total, 128), 1) * (total // owners)
    at = lax.broadcasted_iota(jnp.int32, (total, 128), 0)
    segment = ((at >= low) & (at < low + total // owners)).astype(BF16)
    needed = jnp.dot(hit, segment, preferred_element_type=F32) > 0
    before = lax.broadcasted_iota(jnp.int32, (fields, fields), 0) > lax.broadcasted_iota(jnp.int32, (fields, fields), 1)
    rank = jnp.dot(before.astype(BF16), needed.astype(BF16), preferred_element_type=F32)
    ids = lax.broadcasted_iota(jnp.int32, (fields, 128), 0).astype(F32)
    rows = lax.broadcasted_iota(jnp.int32, (8, 128), 0)
    table = jnp.zeros((8, 128), F32)
    for c in range(CAP):
        chosen = jnp.sum(jnp.where(needed & (rank == c), ids, 0.0), axis=0, keepdims=True)
        table = jnp.where(rows == c, chosen, table)
    table_ref[...] = table.astype(jnp.int32)
    copy = pltpu.make_async_copy(table_ref, scalar_ref, table_sem)
    copy.start()
    copy.wait()
    load.wait()

    def move(d, c, f):
        place = out_ref.at[d, pl.ds(c * lines, lines), :]
        return pltpu.make_async_copy(held_ref.at[f], place, sems.at[d * CAP + c])

    @pl.loop(0, owners)
    def _(d):
        for c in range(CAP):
            move(d, c, scalar_ref[c, d]).start()

    @pl.loop(0, owners)
    def _(d):
        for c in range(CAP):
            move(d, c, 0).wait()


def own_rows(owner, pair_list, embeddings, owners):
    fields, samples, width = embeddings.shape
    out = (owners, CAP * samples, width)
    return pl.pallas_call(
        own_rows_kernel,
        out_shape=(
            jax.ShapeDtypeStruct(out, BF16),
            jax.ShapeDtypeStruct((8, 128), jnp.int32),
        ),
        in_specs=[SMEM, VMEM, HBM],
        out_specs=(HBM, VMEM),
        scratch_shapes=[
            pltpu.VMEM(embeddings.shape, BF16),
            pltpu.SMEM((8, 128), jnp.int32),
            pltpu.SemaphoreType.DMA((owners * CAP,)),
            pltpu.SemaphoreType.DMA,
            pltpu.SemaphoreType.DMA,
        ],
        compiler_params=limit(56 << 20),
        cost_estimate=CHEAP,
    )(owner, pair_list, embeddings)


def far_rows_kernel(ways, count, owner_ref, which_ref, table_ref, *refs):
    sources, outs, (held_ref, sems, load_sems) = refs[:count], refs[count:-3], refs[-3:]
    lines = sources[0].shape[1]

    def move(r, k, c, f):
        place = outs[k].at[c, pl.ds(r * lines, lines), :]
        return pltpu.make_async_copy(held_ref.at[r, f], place, sems.at[r, k * CAP + c])

    def load(r, source):
        return pltpu.make_async_copy(source, held_ref.at[r], load_sems.at[r])

    for r, choices in enumerate(ways):
        for at, source in enumerate(choices):

            @pl.when((len(choices) == 1) | (which_ref[0] == at))
            def _(r=r, source=source):
                load(r, sources[source]).start()

    for r in range(len(ways)):
        load(r, sources[0]).wait()
        for k in range(len(outs)):
            for c in range(CAP):
                move(r, k, c, table_ref[c, owner_ref[0] ^ k]).start()

    for r in range(len(ways)):
        for k in range(len(outs)):
            for c in range(CAP):
                move(r, k, c, 0).wait()


def far_rows(ways, owner, which, table, sources, owners):
    _, lines, width = sources[0].shape
    shape = (CAP, len(ways) * lines, width)
    return pl.pallas_call(
        functools.partial(far_rows_kernel, ways, len(sources)),
        out_shape=[jax.ShapeDtypeStruct(shape, BF16)] * owners,
        in_specs=[SMEM, SMEM, SMEM] + [HBM] * len(sources),
        out_specs=[HBM] * owners,
        scratch_shapes=[
            pltpu.VMEM((len(ways), *sources[0].shape), BF16),
            pltpu.SemaphoreType.DMA((len(ways), owners * CAP)),
            pltpu.SemaphoreType.DMA((len(ways),)),
        ],
        compiler_params=limit(56 << 20),
        cost_estimate=CHEAP,
    )(owner, which, table, *sources)


def forward_kernel(group, slot_ref, width_ref, rows_ref, mats_ref, sums_ref, x_ref, u_ref, acc_ref, mats, sems):
    slots, samples, width = x_ref.shape
    steps = mats.shape[0] // group

    def load(i):
        part = pl.ds(i * group, group)
        return pltpu.make_async_copy(mats_ref.at[part], mats.at[part], sems.at[i])

    for i in range(steps):
        load(i).start()
    columns = lax.broadcasted_iota(jnp.int32, (samples, width), 1)

    @pl.loop(0, slots, unroll=4)
    def _(j):
        x_ref[j] = jnp.where(columns < width_ref[j], rows_ref[j], jnp.zeros_like(rows_ref[j]))
        u_ref[j] = jnp.zeros((samples, width), F32)

    acc_ref[...] = jnp.zeros_like(acc_ref)

    @pl.loop(0, steps)
    def _(i):
        load(i).wait()
        acc = jnp.zeros((samples, width), F32)
        for k in range(group):
            p = i * group + k
            a, b = slot_ref[2 * p], slot_ref[2 * p + 1]
            left, right, mat = x_ref[a], x_ref[b], mats[p]
            projected = jnp.dot(left, mat, preferred_element_type=F32)
            back = lax.dot_general(right, mat, (((1,), (1,)), ((), ())), preferred_element_type=F32)
            acc += projected * right.astype(F32)
            u_ref[b] += projected
            u_ref[a] += back
        acc_ref[...] += acc

    total = acc_ref[:, 0:128]
    for at in range(128, width, 128):
        total = total + acc_ref[:, at : at + 128]
    part = jnp.sum(total.T, axis=0, keepdims=True)
    note = jnp.zeros((NOTE, width), F32)
    for row in range(3):
        piece = part.astype(BF16).astype(F32)
        part = part - piece
        at = lax.broadcasted_iota(jnp.int32, (NOTE, width), 0) == row
        note = jnp.where(at, jnp.concatenate([piece] * (width // samples), axis=1), note)
    lines = CAP * samples

    @pl.loop(0, slots // CAP)
    def _(o):
        for c in range(CAP):
            sums_ref[o, c * samples : (c + 1) * samples, :] = u_ref[o * CAP + c].astype(BF16)
        sums_ref[o, lines : lines + NOTE, :] = note.astype(BF16)


def forward(slot_index, slot_width, rows, mats, group=8):
    slots, samples, width = rows.shape
    sums = (slots // CAP, CAP * samples + NOTE, width)
    return pl.pallas_call(
        functools.partial(forward_kernel, group),
        out_shape=jax.ShapeDtypeStruct(sums, BF16),
        in_specs=[SMEM, SMEM, VMEM, HBM],
        out_specs=VMEM,
        scratch_shapes=[
            pltpu.VMEM(rows.shape, BF16),
            pltpu.VMEM(rows.shape, F32),
            pltpu.VMEM((samples, width), F32),
            pltpu.VMEM(mats.shape, BF16),
            pltpu.SemaphoreType.DMA((mats.shape[0] // group,)),
        ],
        compiler_params=limit(52 << 20),
        cost_estimate=CHEAP,
    )(slot_index, slot_width, rows, mats)


def factor_kernel(back_ref, labels_ref, logit_ref, grad_ref):
    samples = logit_ref.shape[1]
    lines = back_ref.shape[1] - NOTE
    note = jnp.sum(back_ref[:, lines : lines + NOTE, 0:samples].astype(F32), axis=0)
    logit = note[0:1] + note[1:2] + note[2:3]
    logit_ref[...] = logit
    grad = jax.nn.sigmoid(logit) - labels_ref[...].astype(F32)
    for g in range(grad_ref.shape[0]):
        grad_ref[g] = grad


def factor_of(back, labels, groups):
    samples = labels.shape[1]
    return pl.pallas_call(
        factor_kernel,
        out_shape=(jax.ShapeDtypeStruct((1, samples), F32), jax.ShapeDtypeStruct((groups, 1, samples), F32)),
        in_specs=[VMEM, VMEM],
        out_specs=(VMEM, VMEM),
        compiler_params=limit(math.prod(back.shape) * 2),
        cost_estimate=CHEAP,
    )(back, labels)


def emb_grad_kernel(table_ref, width_ref, back_ref, grad_ref, out_ref):
    fields, samples, width = out_ref.shape
    owners = back_ref.shape[0]

    @pl.loop(0, fields)
    def _(f):
        out_ref[f] = jnp.zeros((samples, width), F32)

    @pl.loop(0, owners)
    def _(o):
        for c in range(CAP):
            f = table_ref[c, o]
            out_ref[f] += back_ref[o, c * samples : (c + 1) * samples, :].astype(F32)

    factor = jnp.broadcast_to(grad_ref[0], (128, samples)).T
    factor = jnp.concatenate([factor] * (width // 128), axis=1)
    columns = lax.broadcasted_iota(jnp.int32, (samples, width), 1)

    @pl.loop(0, fields)
    def _(f):
        out_ref[f] = jnp.where(columns < width_ref[f], out_ref[f] * factor, 0.0)


def emb_grad_of(table, own_width, back, grad, fields):
    samples, width = grad.shape[2], back.shape[2]
    return pl.pallas_call(
        emb_grad_kernel,
        out_shape=jax.ShapeDtypeStruct((fields, samples, width), F32),
        in_specs=[SMEM, SMEM, VMEM, VMEM],
        out_specs=VMEM,
        compiler_params=limit(math.prod(back.shape) * 2 + fields * samples * width * 4),
        cost_estimate=CHEAP,
    )(table, own_width, back, grad)


def mat_grad_kernel(ways, chunk, owners, slot_ref, width_ref, which_ref, source_ref, first_ref, owner_ref, grads_ref, own_ref, *refs):
    raws = refs[:owners]
    *links, out_ref, x_ref, t_ref, acc_ref, done_ref, sems, done_sems = refs[owners:]
    group = done_ref.shape[0] // done_sems.shape[0]
    count = len(ways) + 1
    width = x_ref.shape[2]
    slots, samples, _ = own_ref.shape
    kept_lines = links[0].shape[1]
    raw_lines = samples - kept_lines
    pairs, rows, _ = acc_ref.shape
    own_row = lax.broadcasted_iota(jnp.int32, (rows, width), 0) + first_ref[0]
    columns = lax.broadcasted_iota(jnp.int32, (rows, width), 1)
    pick = (columns == own_row).astype(BF16)

    def place(k, low, size):
        return x_ref.at[:, pl.ds(k * samples + low, size), :]

    def store(i):
        part = pl.ds(i * group, group)
        return pltpu.make_async_copy(done_ref.at[part], out_ref.at[part], done_sems.at[i])

    for start in range(0, count, chunk):
        waits = [[] for _ in range(chunk)]
        for k in range(chunk):
            if start + k == 0:
                waits[k].append(pltpu.make_async_copy(own_ref, place(k, 0, samples), sems.at[k, 0]))
                waits[k][-1].start()
                continue
            r = start + k - 1
            for d in range(owners):
                raw = raws[d].at[:, pl.ds(r * raw_lines, raw_lines), :]
                spot = x_ref.at[pl.ds((owner_ref[0] ^ d) * CAP, CAP), pl.ds(k * samples, raw_lines), :]
                waits[k].append(pltpu.make_async_copy(raw, spot, sems.at[k, 2 + d]))
                waits[k][-1].start()
            for at, link in enumerate(ways[r]):

                @pl.when((len(ways[r]) == 1) | (which_ref[0] == at))
                def _(k=k, link=link):
                    pltpu.make_async_copy(links[link], place(k, raw_lines, kept_lines), sems.at[k, 1]).start()

            waits[k].append(pltpu.make_async_copy(links[0], place(k, raw_lines, kept_lines), sems.at[k, 1]))
        for k in range(chunk):
            for copy in waits[k]:
                copy.wait()
            grad = grads_ref[source_ref[start + k]]

            @pl.loop(0, slots, unroll=24)
            def _(j, k=k, grad=grad):
                x = x_ref[j, k * samples : (k + 1) * samples, :]
                turned = lax.dot_general(pick, x, (((1,), (1,)), ((), ())), preferred_element_type=F32)
                t_ref[j, :, k * samples : (k + 1) * samples] = (turned * grad).astype(BF16)

        def term_of(p):
            a, b = slot_ref[2 * p], slot_ref[2 * p + 1]
            term = jnp.dot(t_ref[a], x_ref[b], preferred_element_type=F32)
            return term if start == 0 else term + acc_ref[p]

        if start + chunk < count:

            @pl.loop(0, pairs, unroll=8)
            def _(p, term_of=term_of):
                acc_ref[p] = term_of(p)

            continue

        @pl.loop(0, pairs // group)
        def _(i, term_of=term_of):
            for k in range(group):
                p = i * group + k
                a, b = slot_ref[2 * p], slot_ref[2 * p + 1]
                kept = (own_row < width_ref[a]) & (columns < width_ref[b])
                done_ref[p] = jnp.where(kept, term_of(p), 0.0).astype(BF16)
            store(i).start()

        @pl.loop(0, pairs // group)
        def _(i):
            store(i).wait()


def mat_grad_of(ways, slot_index, slot_width, which, sources, first, owner, grads, own, raw, links, rows):
    slots, samples, width = own.shape
    pairs = slot_index.shape[0] // 2
    chunk = len(ways) + 1
    while chunk * slots * samples * width > (8 << 20) and chunk % 2 == 0:
        chunk //= 2
    size = chunk * slots * samples * (width + rows) * 2 + pairs * rows * width * 6
    return pl.pallas_call(
        functools.partial(mat_grad_kernel, ways, chunk, len(raw)),
        out_shape=jax.ShapeDtypeStruct((pairs, rows, width), BF16),
        in_specs=[SMEM] * 6 + [VMEM] + [HBM] * (1 + len(raw) + len(links)),
        out_specs=HBM,
        scratch_shapes=[
            pltpu.VMEM((slots, chunk * samples, width), BF16),
            pltpu.VMEM((slots, rows, chunk * samples), BF16),
            pltpu.VMEM((pairs, rows, width), F32),
            pltpu.VMEM((pairs, rows, width), BF16),
            pltpu.SemaphoreType.DMA((chunk, 2 + len(raw))),
            pltpu.SemaphoreType.DMA((pairs // 16,)),
        ],
        compiler_params=limit(56 << 20),
        cost_estimate=CHEAP,
    )(slot_index, slot_width, which, sources, first, owner, grads, own, *raw, *links)


def shards(embeddings, field_width, pair_fields, pair_mats, labels):
    owners = lax.axis_size("pair")
    groups = lax.axis_size("dp")
    owner = lax.axis_index("pair")
    group = lax.axis_index("dp")
    fields, samples, width = embeddings.shape
    pairs = pair_mats.shape[0]
    every = owners * fields

    pair_list = pair_fields.T
    field_ids = jnp.arange(fields, dtype=jnp.int32)
    slot_ids = jnp.arange(CAP, dtype=jnp.int32)
    picked, table = own_rows(owner.reshape(1), pair_list, embeddings, owners)

    mine = lax.dynamic_slice_in_dim(pair_list, owner * pairs, pairs, 1)
    all_ids = jnp.arange(every, dtype=jnp.int32)
    hit = mine.T.reshape(-1)[:, None] == all_ids[None, :]
    wanted = jnp.any(hit, axis=0).astype(jnp.int32).reshape(owners, fields)
    place = jnp.sum(jnp.where(field_ids[:, None] > field_ids[None, :], wanted[:, None, :], 0), axis=2)
    slot_of = jnp.arange(owners, dtype=jnp.int32)[:, None] * CAP + place
    slot_index = jnp.sum(jnp.where(hit, slot_of.reshape(-1)[None, :], 0), axis=1)
    taken = (wanted[:, None, :] > 0) & (place[:, None, :] == slot_ids[None, :, None])
    slot_width = jnp.sum(jnp.where(taken, field_width.reshape(owners, 1, fields), 0), axis=2).reshape(-1)
    own_width = lax.dynamic_slice_in_dim(field_width, owner * fields, fields, 0)

    def swap(rows, k, members=range(groups)):
        return lax.ppermute(rows, "dp", [(i, i ^ k) for i in members])

    def chain(own):
        if groups != 4:
            found = [swap(own, k) for k in range(1, groups)]
            yield found
            yield found
            return
        beside, across = swap(own, 1), swap(own, 3)
        yield [beside, across]
        yield [beside, across, swap(beside, 3, (1, 2)), swap(across, 1, (1, 2))]

    def exchange(rows):
        lines = rows.reshape(owners, -1, width)
        return lax.all_to_all(lines, "pair", split_axis=0, concat_axis=0, tiled=True)

    tie = lax.optimization_barrier
    ways = [[0], [1], [2, 3]] if groups == 4 else [[k] for k in range(groups - 1)]
    steps = (1, 3, 2) if groups == 4 else range(1, groups)
    which = ((group == 0) | (group == 3)).astype(jnp.int32).reshape(1)
    sources = jnp.stack([group] + [group ^ k for k in steps]).astype(jnp.int32)

    raw_steps = chain(embeddings[:, :RAW])
    close = next(raw_steps)
    received = exchange(picked).reshape(owners * CAP, samples, width)
    received, close[:] = tie((received, close))
    raw = next(raw_steps)
    kept_steps = chain(received[:, RAW:])
    sums = forward(slot_index, slot_width, received, pair_mats)
    sums, raw = tie((sums, raw))
    back = exchange(sums)
    near_kept = next(kept_steps)
    far = far_rows(ways, owner.reshape(1), which, table, raw, owners)
    first = [k for k in range(2, owners, 2)]
    moved = {k: lax.ppermute(far[k], "pair", [(i, i ^ k) for i in range(owners)]) for k in first}
    rest = [k for k in range(owners - 1, 0, -1) if k not in first]
    if owners == 8:
        moved, far = tie((moved, far))
    moved |= {k: lax.ppermute(far[k], "pair", [(i, i ^ k) for i in range(owners)]) for k in rest}
    far = [moved.get(k, far[k]) for k in range(owners)]
    kept = next(kept_steps)
    back, near_kept[:] = tie((back, near_kept))
    logits, grad = factor_of(back, labels[None, :], groups)
    logits = logits.reshape(samples)
    grads = lax.all_to_all(grad, "dp", split_axis=0, concat_axis=0, tiled=True)
    emb_grad = emb_grad_of(table, own_width, back, grad, fields)
    rows = width // groups
    mat_grad = mat_grad_of(
        ways, slot_index, slot_width, which, sources, (group * rows).reshape(1), owner.reshape(1), grads, received, far, kept, rows
    )
    return (logits, mat_grad, emb_grad)


def solution(mesh):
    in_specs = (P("pair", "dp", None), P(), P(), P("pair", None, None), P("dp"))
    out_specs = (P("dp"), P("pair", "dp", None), P("pair", "dp", None))
    return jax.shard_map(shards, mesh=mesh, in_specs=in_specs, out_specs=out_specs, check_vma=False)
```

```python
import functools
import math

import jax
import jax.numpy as jnp
from jax import lax
from jax.experimental import pallas as pl
from jax.experimental.pallas import tpu as pltpu
from jax.sharding import PartitionSpec as P

CAP = 3
NOTE = 16
RAW = 64
VMEM = pl.BlockSpec(memory_space=pltpu.VMEM)
SMEM = pl.BlockSpec(memory_space=pltpu.SMEM)
HBM = pl.BlockSpec(memory_space=pl.ANY)
F32 = jnp.float32
BF16 = jnp.bfloat16
CHEAP = pl.CostEstimate(flops=0, bytes_accessed=0, transcendentals=0)


def limit(size):
    return pltpu.CompilerParams(vmem_limit_bytes=size + (4 << 20))


def own_rows_kernel(owner_ref, pairs_ref, rows_ref, out_ref, table_ref, held_ref, scalar_ref, sems, table_sem, load_sem):
    fields = rows_ref.shape[0]
    owners = out_ref.shape[0]
    lines, width = out_ref.shape[1] // CAP, out_ref.shape[2]
    total = pairs_ref.shape[1]
    load = pltpu.make_async_copy(rows_ref, held_ref, load_sem)
    load.start()
    local = pairs_ref[...] - owner_ref[0] * fields
    field = lax.broadcasted_iota(jnp.int32, (fields, total), 0)
    hit = ((local[0:1] == field) | (local[1:2] == field)).astype(BF16)
    low = lax.broadcasted_iota(jnp.int32, (total, 128), 1) * (total // owners)
    at = lax.broadcasted_iota(jnp.int32, (total, 128), 0)
    segment = ((at >= low) & (at < low + total // owners)).astype(BF16)
    needed = jnp.dot(hit, segment, preferred_element_type=F32) > 0
    before = lax.broadcasted_iota(jnp.int32, (fields, fields), 0) > lax.broadcasted_iota(jnp.int32, (fields, fields), 1)
    rank = jnp.dot(before.astype(BF16), needed.astype(BF16), preferred_element_type=F32)
    ids = lax.broadcasted_iota(jnp.int32, (fields, 128), 0).astype(F32)
    rows = lax.broadcasted_iota(jnp.int32, (8, 128), 0)
    table = jnp.zeros((8, 128), F32)
    for c in range(CAP):
        chosen = jnp.sum(jnp.where(needed & (rank == c), ids, 0.0), axis=0, keepdims=True)
        table = jnp.where(rows == c, chosen, table)
    table_ref[...] = table.astype(jnp.int32)
    copy = pltpu.make_async_copy(table_ref, scalar_ref, table_sem)
    copy.start()
    copy.wait()
    load.wait()

    def move(d, c, f):
        place = out_ref.at[d, pl.ds(c * lines, lines), :]
        return pltpu.make_async_copy(held_ref.at[f], place, sems.at[d * CAP + c])

    @pl.loop(0, owners)
    def _(d):
        for c in range(CAP):
            move(d, c, scalar_ref[c, d]).start()

    @pl.loop(0, owners)
    def _(d):
        for c in range(CAP):
            move(d, c, 0).wait()


def own_rows(owner, pair_list, embeddings, owners):
    fields, samples, width = embeddings.shape
    out = (owners, CAP * samples, width)
    return pl.pallas_call(
        own_rows_kernel,
        out_shape=(
            jax.ShapeDtypeStruct(out, BF16),
            jax.ShapeDtypeStruct((8, 128), jnp.int32),
        ),
        in_specs=[SMEM, VMEM, HBM],
        out_specs=(HBM, VMEM),
        scratch_shapes=[
            pltpu.VMEM(embeddings.shape, BF16),
            pltpu.SMEM((8, 128), jnp.int32),
            pltpu.SemaphoreType.DMA((owners * CAP,)),
            pltpu.SemaphoreType.DMA,
            pltpu.SemaphoreType.DMA,
        ],
        compiler_params=limit(56 << 20),
        cost_estimate=CHEAP,
    )(owner, pair_list, embeddings)


def far_rows_kernel(ways, count, owner_ref, which_ref, table_ref, *refs):
    sources, outs, (held_ref, sems, load_sems) = refs[:count], refs[count:-3], refs[-3:]
    lines = sources[0].shape[1]

    def move(r, k, c, f):
        place = outs[k].at[c, pl.ds(r * lines, lines), :]
        return pltpu.make_async_copy(held_ref.at[r, f], place, sems.at[r, k * CAP + c])

    def load(r, source):
        return pltpu.make_async_copy(source, held_ref.at[r], load_sems.at[r])

    for r, choices in enumerate(ways):
        for at, source in enumerate(choices):

            @pl.when((len(choices) == 1) | (which_ref[0] == at))
            def _(r=r, source=source):
                load(r, sources[source]).start()

    for r in range(len(ways)):
        load(r, sources[0]).wait()
        for k in range(len(outs)):
            for c in range(CAP):
                move(r, k, c, table_ref[c, owner_ref[0] ^ k]).start()

    for r in range(len(ways)):
        for k in range(len(outs)):
            for c in range(CAP):
                move(r, k, c, 0).wait()


def far_rows(ways, owner, which, table, sources, owners):
    _, lines, width = sources[0].shape
    shape = (CAP, len(ways) * lines, width)
    return pl.pallas_call(
        functools.partial(far_rows_kernel, ways, len(sources)),
        out_shape=[jax.ShapeDtypeStruct(shape, BF16)] * owners,
        in_specs=[SMEM, SMEM, SMEM] + [HBM] * len(sources),
        out_specs=[HBM] * owners,
        scratch_shapes=[
            pltpu.VMEM((len(ways), *sources[0].shape), BF16),
            pltpu.SemaphoreType.DMA((len(ways), owners * CAP)),
            pltpu.SemaphoreType.DMA((len(ways),)),
        ],
        compiler_params=limit(56 << 20),
        cost_estimate=CHEAP,
    )(owner, which, table, *sources)


def forward_kernel(group, slot_ref, width_ref, rows_ref, mats_ref, sums_ref, x_ref, u_ref, acc_ref, mats, sems):
    slots, samples, width = x_ref.shape
    steps = mats.shape[0] // group

    def load(i):
        part = pl.ds(i * group, group)
        return pltpu.make_async_copy(mats_ref.at[part], mats.at[part], sems.at[i])

    for i in range(steps):
        load(i).start()
    columns = lax.broadcasted_iota(jnp.int32, (samples, width), 1)

    @pl.loop(0, slots, unroll=4)
    def _(j):
        x_ref[j] = jnp.where(columns < width_ref[j], rows_ref[j], jnp.zeros_like(rows_ref[j]))
        u_ref[j] = jnp.zeros((samples, width), F32)

    acc_ref[...] = jnp.zeros_like(acc_ref)

    @pl.loop(0, steps)
    def _(i):
        load(i).wait()
        acc = jnp.zeros((samples, width), F32)
        for k in range(group):
            p = i * group + k
            a, b = slot_ref[2 * p], slot_ref[2 * p + 1]
            left, right, mat = x_ref[a], x_ref[b], mats[p]
            projected = jnp.dot(left, mat, preferred_element_type=F32)
            back = lax.dot_general(right, mat, (((1,), (1,)), ((), ())), preferred_element_type=F32)
            acc += projected * right.astype(F32)
            u_ref[b] += projected
            u_ref[a] += back
        acc_ref[...] += acc

    total = acc_ref[:, 0:128]
    for at in range(128, width, 128):
        total = total + acc_ref[:, at : at + 128]
    part = jnp.sum(total.T, axis=0, keepdims=True)
    note = jnp.zeros((NOTE, width), F32)
    for row in range(3):
        piece = part.astype(BF16).astype(F32)
        part = part - piece
        at = lax.broadcasted_iota(jnp.int32, (NOTE, width), 0) == row
        note = jnp.where(at, jnp.concatenate([piece] * (width // samples), axis=1), note)
    lines = CAP * samples

    @pl.loop(0, slots // CAP)
    def _(o):
        for c in range(CAP):
            sums_ref[o, c * samples : (c + 1) * samples, :] = u_ref[o * CAP + c].astype(BF16)
        sums_ref[o, lines : lines + NOTE, :] = note.astype(BF16)


def forward(slot_index, slot_width, rows, mats, group=12):
    slots, samples, width = rows.shape
    sums = (slots // CAP, CAP * samples + NOTE, width)
    return pl.pallas_call(
        functools.partial(forward_kernel, group),
        out_shape=jax.ShapeDtypeStruct(sums, BF16),
        in_specs=[SMEM, SMEM, VMEM, HBM],
        out_specs=VMEM,
        scratch_shapes=[
            pltpu.VMEM(rows.shape, BF16),
            pltpu.VMEM(rows.shape, F32),
            pltpu.VMEM((samples, width), F32),
            pltpu.VMEM(mats.shape, BF16),
            pltpu.SemaphoreType.DMA((mats.shape[0] // group,)),
        ],
        compiler_params=limit(52 << 20),
        cost_estimate=CHEAP,
    )(slot_index, slot_width, rows, mats)


def factor_kernel(back_ref, labels_ref, logit_ref, grad_ref):
    samples = logit_ref.shape[1]
    lines = back_ref.shape[1] - NOTE
    note = jnp.sum(back_ref[:, lines : lines + NOTE, 0:samples].astype(F32), axis=0)
    logit = note[0:1] + note[1:2] + note[2:3]
    logit_ref[...] = logit
    grad = jax.nn.sigmoid(logit) - labels_ref[...].astype(F32)
    for g in range(grad_ref.shape[0]):
        grad_ref[g] = grad


def factor_of(back, labels, groups):
    samples = labels.shape[1]
    return pl.pallas_call(
        factor_kernel,
        out_shape=(jax.ShapeDtypeStruct((1, samples), F32), jax.ShapeDtypeStruct((groups, 1, samples), F32)),
        in_specs=[VMEM, VMEM],
        out_specs=(VMEM, VMEM),
        compiler_params=limit(math.prod(back.shape) * 2),
        cost_estimate=CHEAP,
    )(back, labels)


def emb_grad_kernel(table_ref, width_ref, back_ref, grad_ref, out_ref):
    fields, samples, width = out_ref.shape
    owners = back_ref.shape[0]

    @pl.loop(0, fields)
    def _(f):
        out_ref[f] = jnp.zeros((samples, width), F32)

    @pl.loop(0, owners)
    def _(o):
        for c in range(CAP):
            f = table_ref[c, o]
            out_ref[f] += back_ref[o, c * samples : (c + 1) * samples, :].astype(F32)

    factor = jnp.broadcast_to(grad_ref[0], (128, samples)).T
    factor = jnp.concatenate([factor] * (width // 128), axis=1)
    columns = lax.broadcasted_iota(jnp.int32, (samples, width), 1)

    @pl.loop(0, fields)
    def _(f):
        out_ref[f] = jnp.where(columns < width_ref[f], out_ref[f] * factor, 0.0)


def emb_grad_of(table, own_width, back, grad, fields):
    samples, width = grad.shape[2], back.shape[2]
    return pl.pallas_call(
        emb_grad_kernel,
        out_shape=jax.ShapeDtypeStruct((fields, samples, width), F32),
        in_specs=[SMEM, SMEM, VMEM, VMEM],
        out_specs=VMEM,
        compiler_params=limit(math.prod(back.shape) * 2 + fields * samples * width * 4),
        cost_estimate=CHEAP,
    )(table, own_width, back, grad)


def mat_grad_kernel(ways, chunk, owners, slot_ref, width_ref, which_ref, source_ref, first_ref, owner_ref, grads_ref, own_ref, *refs):
    raws = refs[:owners]
    *links, out_ref, x_ref, t_ref, acc_ref, done_ref, sems, done_sems = refs[owners:]
    group = done_ref.shape[0] // done_sems.shape[0]
    count = len(ways) + 1
    width = x_ref.shape[2]
    slots, samples, _ = own_ref.shape
    kept_lines = links[0].shape[1]
    raw_lines = samples - kept_lines
    pairs, rows, _ = acc_ref.shape
    own_row = lax.broadcasted_iota(jnp.int32, (rows, width), 0) + first_ref[0]
    columns = lax.broadcasted_iota(jnp.int32, (rows, width), 1)
    pick = (columns == own_row).astype(BF16)

    def place(k, low, size):
        return x_ref.at[:, pl.ds(k * samples + low, size), :]

    def store(i):
        part = pl.ds(i * group, group)
        return pltpu.make_async_copy(done_ref.at[part], out_ref.at[part], done_sems.at[i])

    for start in range(0, count, chunk):
        waits = [[] for _ in range(chunk)]
        for k in range(chunk):
            if start + k == 0:
                waits[k].append(pltpu.make_async_copy(own_ref, place(k, 0, samples), sems.at[k, 0]))
                waits[k][-1].start()
                continue
            r = start + k - 1
            for d in range(owners):
                raw = raws[d].at[:, pl.ds(r * raw_lines, raw_lines), :]
                spot = x_ref.at[pl.ds((owner_ref[0] ^ d) * CAP, CAP), pl.ds(k * samples, raw_lines), :]
                waits[k].append(pltpu.make_async_copy(raw, spot, sems.at[k, 2 + d]))
                waits[k][-1].start()
            for at, link in enumerate(ways[r]):

                @pl.when((len(ways[r]) == 1) | (which_ref[0] == at))
                def _(k=k, link=link):
                    pltpu.make_async_copy(links[link], place(k, raw_lines, kept_lines), sems.at[k, 1]).start()

            waits[k].append(pltpu.make_async_copy(links[0], place(k, raw_lines, kept_lines), sems.at[k, 1]))
        for k in range(chunk):
            for copy in waits[k]:
                copy.wait()
            grad = grads_ref[source_ref[start + k]]

            @pl.loop(0, slots, unroll=24)
            def _(j, k=k, grad=grad):
                x = x_ref[j, k * samples : (k + 1) * samples, :]
                turned = lax.dot_general(pick, x, (((1,), (1,)), ((), ())), preferred_element_type=F32)
                t_ref[j, :, k * samples : (k + 1) * samples] = (turned * grad).astype(BF16)

        def term_of(p):
            a, b = slot_ref[2 * p], slot_ref[2 * p + 1]
            term = jnp.dot(t_ref[a], x_ref[b], preferred_element_type=F32)
            return term if start == 0 else term + acc_ref[p]

        if start + chunk < count:

            @pl.loop(0, pairs, unroll=8)
            def _(p, term_of=term_of):
                acc_ref[p] = term_of(p)

            continue

        @pl.loop(0, pairs // group)
        def _(i, term_of=term_of):
            for k in range(group):
                p = i * group + k
                a, b = slot_ref[2 * p], slot_ref[2 * p + 1]
                kept = (own_row < width_ref[a]) & (columns < width_ref[b])
                done_ref[p] = jnp.where(kept, term_of(p), 0.0).astype(BF16)
            store(i).start()

        @pl.loop(0, pairs // group)
        def _(i):
            store(i).wait()


def mat_grad_of(ways, slot_index, slot_width, which, sources, first, owner, grads, own, raw, links, rows):
    slots, samples, width = own.shape
    pairs = slot_index.shape[0] // 2
    chunk = len(ways) + 1
    while chunk * slots * samples * width > (8 << 20) and chunk % 2 == 0:
        chunk //= 2
    size = chunk * slots * samples * (width + rows) * 2 + pairs * rows * width * 6
    return pl.pallas_call(
        functools.partial(mat_grad_kernel, ways, chunk, len(raw)),
        out_shape=jax.ShapeDtypeStruct((pairs, rows, width), BF16),
        in_specs=[SMEM] * 6 + [VMEM] + [HBM] * (1 + len(raw) + len(links)),
        out_specs=HBM,
        scratch_shapes=[
            pltpu.VMEM((slots, chunk * samples, width), BF16),
            pltpu.VMEM((slots, rows, chunk * samples), BF16),
            pltpu.VMEM((pairs, rows, width), F32),
            pltpu.VMEM((pairs, rows, width), BF16),
            pltpu.SemaphoreType.DMA((chunk, 2 + len(raw))),
            pltpu.SemaphoreType.DMA((pairs // 16,)),
        ],
        compiler_params=limit(56 << 20),
        cost_estimate=CHEAP,
    )(slot_index, slot_width, which, sources, first, owner, grads, own, *raw, *links)


def shards(embeddings, field_width, pair_fields, pair_mats, labels):
    owners = lax.axis_size("pair")
    groups = lax.axis_size("dp")
    owner = lax.axis_index("pair")
    group = lax.axis_index("dp")
    fields, samples, width = embeddings.shape
    pairs = pair_mats.shape[0]
    every = owners * fields

    pair_list = pair_fields.T
    field_ids = jnp.arange(fields, dtype=jnp.int32)
    slot_ids = jnp.arange(CAP, dtype=jnp.int32)
    picked, table = own_rows(owner.reshape(1), pair_list, embeddings, owners)

    mine = lax.dynamic_slice_in_dim(pair_list, owner * pairs, pairs, 1)
    all_ids = jnp.arange(every, dtype=jnp.int32)
    hit = mine.T.reshape(-1)[:, None] == all_ids[None, :]
    wanted = jnp.any(hit, axis=0).astype(jnp.int32).reshape(owners, fields)
    place = jnp.sum(jnp.where(field_ids[:, None] > field_ids[None, :], wanted[:, None, :], 0), axis=2)
    slot_of = jnp.arange(owners, dtype=jnp.int32)[:, None] * CAP + place
    slot_index = jnp.sum(jnp.where(hit, slot_of.reshape(-1)[None, :], 0), axis=1)
    taken = (wanted[:, None, :] > 0) & (place[:, None, :] == slot_ids[None, :, None])
    slot_width = jnp.sum(jnp.where(taken, field_width.reshape(owners, 1, fields), 0), axis=2).reshape(-1)
    own_width = lax.dynamic_slice_in_dim(field_width, owner * fields, fields, 0)

    def swap(rows, k, members=range(groups)):
        return lax.ppermute(rows, "dp", [(i, i ^ k) for i in members])

    def chain(own):
        if groups != 4:
            found = [swap(own, k) for k in range(1, groups)]
            yield found
            yield found
            return
        beside, across = swap(own, 1), swap(own, 3)
        yield [beside, across]
        yield [beside, across, swap(beside, 3, (1, 2)), swap(across, 1, (1, 2))]

    def exchange(rows):
        lines = rows.reshape(owners, -1, width)
        return lax.all_to_all(lines, "pair", split_axis=0, concat_axis=0, tiled=True)

    tie = lax.optimization_barrier
    ways = [[0], [1], [2, 3]] if groups == 4 else [[k] for k in range(groups - 1)]
    steps = (1, 3, 2) if groups == 4 else range(1, groups)
    which = ((group == 0) | (group == 3)).astype(jnp.int32).reshape(1)
    sources = jnp.stack([group] + [group ^ k for k in steps]).astype(jnp.int32)

    raw_steps = chain(embeddings[:, :RAW])
    close = next(raw_steps)
    received = exchange(picked).reshape(owners * CAP, samples, width)
    raw = next(raw_steps)
    kept_steps = chain(received[:, RAW:])
    sums = forward(slot_index, slot_width, received, pair_mats)
    sums, raw = tie((sums, raw))
    back = exchange(sums)
    near_kept = next(kept_steps)
    far = far_rows(ways, owner.reshape(1), which, table, raw, owners)
    first = [k for k in range(2, owners, 2)]
    moved = {k: lax.ppermute(far[k], "pair", [(i, i ^ k) for i in range(owners)]) for k in first}
    rest = [k for k in range(owners - 1, 0, -1) if k not in first]
    if owners == 8:
        moved, far = tie((moved, far))
    moved |= {k: lax.ppermute(far[k], "pair", [(i, i ^ k) for i in range(owners)]) for k in rest}
    far = [moved.get(k, far[k]) for k in range(owners)]
    kept = next(kept_steps)
    back, near_kept[:] = tie((back, near_kept))
    logits, grad = factor_of(back, labels[None, :], groups)
    logits = logits.reshape(samples)
    grads = lax.all_to_all(grad, "dp", split_axis=0, concat_axis=0, tiled=True)
    emb_grad = emb_grad_of(table, own_width, back, grad, fields)
    rows = width // groups
    mat_grad = mat_grad_of(
        ways, slot_index, slot_width, which, sources, (group * rows).reshape(1), owner.reshape(1), grads, received, far, kept, rows
    )
    return (logits, mat_grad, emb_grad)


def solution(mesh):
    in_specs = (P("pair", "dp", None), P(), P(), P("pair", None, None), P("dp"))
    out_specs = (P("dp"), P("pair", "dp", None), P("pair", "dp", None))
    return jax.shard_map(shards, mesh=mesh, in_specs=in_specs, out_specs=out_specs, check_vma=False)
```
